32 devices in a mesh: brow: 4 (over z), bcol: 8 (over y, x, core).
Axes of the slice: x: 2, y: 2, z: 4, core: 2. Of those that a mesh axis runs over, the one named last changes fastest.
Arguments:
- blocks: bfloat16 [4, 8, 40, 256, 256], P('brow', 'bcol'), may hold values from -6 to 6
- pattern_rows: int32 [4, 8, 40], P('brow', 'bcol'), may hold values from 0 to 23
- pattern_cols: int32 [4, 8, 40], P('brow', 'bcol'), may hold values from 0 to 11
- live_count: int32 [4, 8], P('brow', 'bcol'), may hold values from 10 to 40, as said below
- degree_scale: float32 [24576], P(('brow', 'bcol')), may hold values from 0.03125 to 0.125
- eigen_block: float32 [32, 24576], P(None, ('brow', 'bcol')), may hold values from -6 to 6
- direction: float32 [32, 24576], P(None, ('brow', 'bcol')), may hold values from -6 to 6
- cutoff: float32 [1], replicated, may hold values from 0.9 to 1
Outputs:
- eigen_next: float32 [32, 24576], P(None, ('brow', 'bcol'))
- direction_next: float32 [32, 24576], P(None, ('brow', 'bcol'))
- residual: float32 [32, 24576], P(None, ('brow', 'bcol'))
- direction_image: float32 [32, 24576], P(None, ('brow', 'bcol'))
The draws below stay inside these ranges and needn't reach their ends.
Inputs may be any that keep to these rules, and one draw needn't show every extreme that they name: `live_count`: some owner uses all 40 slots in every draw.
All inputs are finite; a program needn't handle non-finite values.
Results may differ from the reference program's by a relative error of at most 0.033.
Values may be sent and summed in bfloat16 or wider, within the bound.
A program may use at most 64 MiB of HBM per device.

```python
import math
import jax
import jax.numpy as jnp
from jax import lax

BS = 256
K = 32
PIECE = 3
ITERS = 2
NS_STEPS = 8
SLOTS = 40
BROWS_LOC = 24
BCOLS_LOC = 12
DOCS = 24576
N_BROW = 4
N_BCOL = 8


def draw_live_count(key, part):
    key = jax.random.fold_in(key, 11)
    first_key, second_key, third_key = jax.random.split(key, 3)
    spread = SLOTS - SLOTS // 4
    owners = N_BROW * N_BCOL
    left_part = jax.random.randint(first_key, (owners,), 0, spread + 1)
    right_part = jax.random.randint(second_key, (owners,), 0, spread + 1)
    counts = SLOTS // 4 + left_part * right_part // spread
    busiest = jax.random.randint(third_key, (), 0, owners)
    counts = jnp.where(jnp.arange(owners) == busiest, SLOTS, counts)
    return counts.reshape(N_BROW, N_BCOL).astype(jnp.int32)


def with_ends(entries, stream_key, low, top_value):
    longest = entries.shape.index(max(entries.shape))
    spots = []
    for shift in (0, 1):
        where = [jax.random.randint(jax.random.fold_in(stream_key, axis), (), 0, length) for axis, length in enumerate(entries.shape)]
        where[longest] = (where[longest] + shift) % entries.shape[longest]
        spots.append(tuple(where))
    return entries.at[spots[0]].set(low).at[spots[1]].set(top_value)


def block_levels(key, extent, cuts, low, high):
    gain = 1.0
    for dim, parts in cuts:
        draws = jax.random.uniform(jax.random.fold_in(jax.random.fold_in(key, 6), dim), (parts,), jnp.float32, low / len(cuts), high / len(cuts))
        gain = gain * jnp.repeat(jnp.exp(draws), extent[dim] // parts).reshape((-1,) + (1,) * (len(extent) - 1 - dim))
    return gain


def noise(own_key, extent, width, most, cuts=(), held_as=jnp.bfloat16):
    factor_of = block_levels(own_key, extent, cuts, -0.22, 0.18) if cuts else 1.0
    values = jax.random.normal(own_key, extent, jnp.float32) * width * factor_of
    return jnp.minimum(jnp.maximum(values, -most), most).astype(held_as)


def setup_inputs(seed: int = 0) -> dict:
    arg_keys = jax.random.split(jax.random.key(seed), 9)
    return {
        "blocks": noise(arg_keys[0], (N_BROW, N_BCOL, SLOTS, BS, BS), 1.0, 6.0, ((0, 4), (1, 8))),
        "pattern_rows": with_ends(jax.random.randint(arg_keys[1], (N_BROW, N_BCOL, SLOTS), 0, BROWS_LOC), jax.random.fold_in(arg_keys[1], 1), 0, BROWS_LOC - 1).astype(jnp.int32),
        "pattern_cols": with_ends(jax.random.randint(arg_keys[2], (N_BROW, N_BCOL, SLOTS), 0, BCOLS_LOC), jax.random.fold_in(arg_keys[2], 1), 0, BCOLS_LOC - 1).astype(jnp.int32),
        "live_count": draw_live_count(jax.random.fold_in(arg_keys[8], 71), 0),
        "degree_scale": jnp.clip(jnp.exp(math.log(0.125) - 1.3862944 * jax.random.uniform(arg_keys[4], (DOCS,), jnp.float32) ** block_levels(arg_keys[4], (DOCS,), ((0, 32),), -0.2, 0.2)), 0.03125, 0.125),
        "eigen_block": noise(arg_keys[5], (K, DOCS), 1.0, 6.0, ((1, 32),), jnp.float32),
        "direction": noise(arg_keys[6], (K, DOCS), 1.0, 6.0, ((1, 32),), jnp.float32),
        "cutoff": jnp.clip(jax.random.uniform(arg_keys[7], (1,), jnp.float32, 0.9, 1.0), 0.9, 1.0),
    }


def graph_product(blocks, pattern_rows, pattern_cols, live_count, stack_rows):
    columns = stack_rows.shape[0]
    pieces = stack_rows.reshape(columns, N_BROW, N_BCOL, PIECE * BS)
    slot_index = jnp.arange(SLOTS)

    def per_owner(row_owner):

        def per_column(total, col_owner):
            panel = jnp.take(pieces, col_owner, axis=2).reshape(columns, N_BROW * PIECE, BS)
            picked = jnp.take(panel, pattern_cols[row_owner, col_owner], axis=1).astype(jnp.float32)
            products = jnp.einsum('sab,csb->csa', blocks[row_owner, col_owner].astype(jnp.float32), picked)
            kept_mask = (slot_index < live_count[row_owner, col_owner]).astype(jnp.float32)
            partial_value = jnp.zeros((columns, N_BCOL * PIECE, BS), jnp.float32)
            partial_value = partial_value.at[:, pattern_rows[row_owner, col_owner]].add(products * kept_mask[None, :, None])
            partial_value = lax.optimization_barrier(partial_value.astype(jnp.bfloat16)).astype(jnp.float32)
            return (total + partial_value.reshape(columns, -1), None)
        start_sum = jnp.zeros((columns, N_BCOL * PIECE * BS), jnp.float32)
        total, _ = lax.scan(per_column, start_sum, jnp.arange(N_BCOL))
        return total
    owners = lax.map(per_owner, jnp.arange(N_BROW))
    return jnp.transpose(owners, (1, 0, 2)).reshape(columns, -1)

def highest_dot(left, right):
    return jnp.dot(left, right, precision=lax.Precision.HIGHEST)

def solve_quotient(gram_x, rayleigh_x):
    lower = jnp.linalg.cholesky(gram_x)
    middle = lax.linalg.triangular_solve(lower, rayleigh_x, left_side=True, lower=True)
    return lax.linalg.triangular_solve(lower, middle, left_side=True, lower=True, transpose_a=True)

def ritz_coefficients(gram_b, gram_a, cutoff, wanted):
    lower = jnp.linalg.cholesky(gram_b)
    first = lax.linalg.triangular_solve(lower, gram_a, left_side=True, lower=True)
    small = lax.linalg.triangular_solve(lower, first.T, left_side=True, lower=True)
    identity = jnp.eye(small.shape[0], dtype=jnp.float32)
    shifted = cutoff[0] * identity - small
    sign_now = shifted / jnp.sqrt(jnp.sum(shifted * shifted) + 1e-06)
    for sweep_index in range(NS_STEPS):
        sign_now = 1.5 * sign_now - 0.5 * highest_dot(sign_now, highest_dot(sign_now, sign_now))
    projector = 0.5 * (identity + sign_now)
    inner = highest_dot(projector, lower.T[:, :wanted])
    return lax.linalg.triangular_solve(lower, inner, left_side=True, lower=True, transpose_a=True)

def reference(blocks, pattern_rows, pattern_cols, live_count, degree_scale, eigen_block, direction, cutoff):
    wanted = eigen_block.shape[0]
    vectors, searches = (eigen_block, direction)
    for section_index in range(ITERS + 1):
        panel = (degree_scale * jnp.concatenate([vectors, searches], 0)).astype(jnp.bfloat16)
        image = graph_product(blocks, pattern_rows, pattern_cols, live_count, panel)
        image_x = vectors - degree_scale * image[:wanted]
        image_p = searches - degree_scale * image[wanted:]
        gram_x = highest_dot(vectors, vectors.T)
        rayleigh_x = highest_dot(vectors, image_x.T)
        quotient = solve_quotient(gram_x, rayleigh_x)
        remainder = image_x - highest_dot(quotient.T, vectors)
        if section_index < ITERS:
            residual_panel = (degree_scale * remainder).astype(jnp.bfloat16)
            image_r = remainder - degree_scale * graph_product(blocks, pattern_rows, pattern_cols, live_count, residual_panel)
            basis = jnp.concatenate([vectors, remainder, searches], 0)
            basis_image = jnp.concatenate([image_x, image_r, image_p], 0)
            gram_b = highest_dot(basis, basis.T)
            cross = highest_dot(basis, basis_image.T)
            gram_a = 0.5 * (cross + cross.T)
            coeffs = ritz_coefficients(gram_b, gram_a, cutoff, wanted)
            row_mask = (jnp.arange(coeffs.shape[0]) >= wanted).astype(jnp.float32)
            vectors_new = highest_dot(coeffs.T, basis)
            searches = highest_dot((coeffs * row_mask[:, None]).T, basis)
            vectors = vectors_new
    return (vectors, searches, remainder, image_p)
```

```python
import functools

import jax
import jax.numpy as jnp
from jax import lax
from jax.experimental import pallas as pl
from jax.experimental.pallas import tpu as pltpu
from jax.sharding import PartitionSpec as P

ITERS = 2
NS_STEPS = 8
MESH = pl.DeviceIdType.MESH
LANES = 128


def dot(left, right):
    return jnp.dot(
        left, right, precision=lax.Precision.HIGHEST, preferred_element_type=jnp.float32
    )


def dot_nt(left, right, precision=lax.Precision.HIGHEST):
    return lax.dot_general(
        left,
        right,
        (((1,), (1,)), ((), ())),
        precision=precision,
        preferred_element_type=jnp.float32,
    )


def grid_ids(rows):
    shape = (rows, LANES)
    return (
        lax.broadcasted_iota(jnp.int32, shape, 0),
        lax.broadcasted_iota(jnp.int32, shape, 1),
    )


def pad_rows(value, before=0):
    parts = [value, jnp.zeros((LANES - before - value.shape[0], LANES), jnp.float32)]
    if before:
        parts.insert(0, jnp.zeros((before, LANES), jnp.float32))
    return jnp.concatenate(parts, 0)


def inverse(matrix):
    side = matrix.shape[0]
    row_id, col_id = grid_ids(side)

    def sweep(k, now):
        at_row, at_col = row_id == k, col_id == k
        row = jnp.sum(jnp.where(at_row, now, 0.0), axis=0, keepdims=True)
        col = jnp.sum(jnp.where(at_col, now, 0.0), axis=1, keepdims=True)
        pivot = jnp.sum(jnp.where(at_row, col, 0.0), axis=0, keepdims=True)
        scale = 1.0 / pivot
        scaled_row = row * scale
        out = jnp.where(at_col, col * scale, now - col * scaled_row)
        out = jnp.where(at_row, jnp.where(at_col, -scale, scaled_row), out)
        return out

    return -lax.fori_loop(0, side, sweep, matrix)


def extend_inverse(known, border, offset):
    side = border.shape[0]
    row_id, col_id = grid_ids(side)
    placed = (col_id == row_id + offset).astype(jnp.float32)
    edge = pad_rows(placed - dot(border, known))
    middle = inverse(dot_nt(border, edge))
    return known + dot(edge.T, pad_rows(dot(middle, edge)))


def body(
    n_row, n_col, piece, slots, wanted,
    tables, cutoff, blocks_hbm, scale_ref, eigen_ref, direction_ref,
    out_x, out_p, out_r, out_ip,
    blocks, basis, image, work, sums,
    gather_x, gather_r, part_x, part_r, land_x, land_r, cols_x, rows_x,
    block_sem, gx_send, gx_recv, gr_send, gr_recv, px_send, px_recv, pr_send, pr_recv,
    c_send, c_recv, r_send, r_recv,
):
    me_row, me_col = lax.axis_index("brow"), lax.axis_index("bcol")
    side = blocks.shape[-1]
    block_copy = pltpu.make_async_copy(blocks_hbm, blocks, block_sem)
    block_copy.start()

    def row_peer(step):
        return lax.rem(me_row + step, n_row)

    def col_peer(step):
        return lax.rem(me_col + step, n_col)

    barrier = pltpu.get_barrier_semaphore()
    for step in range(1, n_row):
        pl.semaphore_signal(
            barrier, inc=1, device_id=(row_peer(step), me_col), device_id_type=MESH
        )
    for step in range(1, n_col):
        pl.semaphore_signal(
            barrier, inc=1, device_id=(me_row, col_peer(step)), device_id_type=MESH
        )

    basis[0:wanted] = eigen_ref[...]
    basis[wanted : 2 * wanted] = direction_ref[...]
    basis[2 * wanted :] = jnp.zeros((LANES - 2 * wanted, piece * side), jnp.float32)
    image[...] = jnp.zeros(image.shape, jnp.float32)
    sums[slots] = jnp.zeros(sums.shape[1:], jnp.float32)

    pl.semaphore_wait(barrier, n_row + n_col - 2)
    row_id, col_id = grid_ids(LANES)
    eye = jnp.where((row_id == col_id) & (row_id < 3 * wanted), 1.0, 0.0)

    def remote(src, dst, send, recv, device):
        return pltpu.make_async_remote_copy(
            src_ref=src, dst_ref=dst, send_sem=send, recv_sem=recv,
            device_id=device, device_id_type=MESH,
        )

    def spot(p):
        return slice(p * side, (p + 1) * side)

    def apply_graph(turn, first, count, gather, part, land, sems, wait_blocks):
        g_send, g_recv, p_send, p_recv = sems
        rows = slice(first, first + count)
        mine = pl.ds(me_row * piece, piece)
        for p in range(piece):
            gather[turn, me_row * piece + p] = (
                scale_ref[:, spot(p)] * basis[rows, spot(p)]
            ).astype(jnp.bfloat16)
        copies = []
        for step in range(1, n_row):
            copies.append(
                remote(
                    gather.at[turn, mine], gather.at[turn, mine],
                    g_send.at[turn, step - 1], g_recv.at[turn, step - 1],
                    (row_peer(step), me_col),
                )
            )
            copies[-1].start()
        if wait_blocks is not None:
            wait_blocks()
        for copy in copies:
            copy.wait()

        def move(k, carry):
            work[k, 0:count] = gather[turn, k]
            return carry

        lax.fori_loop(0, n_row * piece, move, 0)

        def slot(s, carry):
            product = dot_nt(
                work[tables[s], 0:count], blocks[s], precision=lax.Precision.DEFAULT
            )
            sums[s, 0:count] = product + sums[tables[slots + s], 0:count]
            return carry

        lax.fori_loop(0, slots, slot, 0, unroll=4)

        def row_sum(owner, p):
            return sums[tables[2 * slots + owner * piece + p], 0:count]

        copies = []
        for step in range(1, n_col):
            owner = col_peer(step)
            for p in range(piece):
                part[turn, step - 1, p] = row_sum(owner, p).astype(jnp.bfloat16)
            copies.append(
                remote(
                    part.at[turn, step - 1], land.at[turn, step - 1],
                    p_send.at[turn, step - 1], p_recv.at[turn, step - 1],
                    (me_row, owner),
                )
            )
            copies[-1].start()
        for copy in copies:
            copy.wait()
        for p in range(piece):
            total = row_sum(me_col, p)
            for step in range(1, n_col):
                total = total + land[turn, step - 1, p].astype(jnp.float32)
            image[rows, spot(p)] = basis[rows, spot(p)] - scale_ref[:, spot(p)] * total

    def add_up(turn, value):
        for land, send, recv, count, me in (
            (cols_x, c_send, c_recv, n_col, me_col),
            (rows_x, r_send, r_recv, n_row, me_row),
        ):
            land[turn, me] = value
            copies = []
            for step in range(1, count):
                device = (
                    (me_row, col_peer(step)) if land is cols_x else (row_peer(step), me_col)
                )
                copies.append(
                    remote(
                        land.at[turn, me], land.at[turn, me],
                        send.at[turn, step - 1], recv.at[turn, step - 1], device,
                    )
                )
                copies[-1].start()
            for copy in copies:
                copy.wait()
            value = land[turn, 0]
            for k in range(1, count):
                value = value + land[turn, k]
        return value

    pair = slice(0, 2 * wanted)
    third = slice(2 * wanted, 3 * wanted)
    x_sems = (gx_send, gx_recv, px_send, px_recv)
    r_sems = (gr_send, gr_recv, pr_send, pr_recv)

    def section(turn, carry):
        def wait_blocks():
            @pl.when(turn == 0)
            def _():
                block_copy.wait()

        apply_graph(turn, 0, 2 * wanted, gather_x, part_x, land_x, x_sems, wait_blocks)
        both = jnp.concatenate([basis[pair], image[pair]], 0)
        grams = add_up(2 * turn, dot_nt(basis[pair], both))
        flipped = pad_rows(grams).T
        narrow = grid_ids(wanted)[1] < wanted
        gram_inv = pad_rows(inverse(jnp.where(narrow, grams[0:wanted], 0.0)))
        rayleigh_t = jnp.where(narrow, flipped[2 * wanted : 3 * wanted], 0.0)
        quotient_t = dot(rayleigh_t, gram_inv)
        basis[third] = image[0:wanted] - dot(quotient_t, basis[...])

        @pl.when(turn < ITERS)
        def _():
            apply_graph(
                turn, 2 * wanted, wanted, gather_r, part_r, land_r, r_sems, None
            )
            half = grid_ids(wanted)[1] < 2 * wanted
            pair_inv = extend_inverse(
                gram_inv, jnp.where(half, grams[wanted : 2 * wanted], 0.0), wanted
            )
            cross_t = pad_rows(flipped[2 * wanted :])
            residual = basis[third]
            border = add_up(
                2 * turn + 1,
                jnp.concatenate(
                    [
                        dot_nt(residual, basis[...]),
                        0.5
                        * (dot_nt(image[third], basis[...]) + dot_nt(residual, image[...])),
                    ],
                    0,
                ),
            )
            full_inv = extend_inverse(pair_inv, border[0:wanted], 2 * wanted)
            low = pad_rows(border[wanted:], 2 * wanted)
            gram_a = (
                0.5 * (cross_t + cross_t.T)
                + low
                + jnp.where(row_id < 2 * wanted, low.T, 0.0)
            )
            shifted = cutoff[0] * eye - dot(gram_a, full_inv)
            square = dot(shifted, shifted)
            trace = jnp.sum(
                jnp.sum(jnp.where(row_id == col_id, square, 0.0), axis=1, keepdims=True),
                axis=0,
                keepdims=True,
            )
            norm = 1.0 / jnp.sqrt(trace + 1e-06)
            sign = (1.5 * norm) * shifted - (0.5 * norm) * dot(
                shifted * norm, square * norm
            )

            def newton(_, now):
                return 1.5 * now - 0.5 * dot(now, dot(now, now))

            sign = lax.fori_loop(0, NS_STEPS - 1, newton, sign)
            coeffs = 0.5 * (eye + sign)[0:wanted]
            mixed = jnp.concatenate([coeffs, jnp.where(narrow, 0.0, coeffs)], 0)
            basis[pair] = dot(mixed, basis[...])

        return carry

    lax.fori_loop(0, ITERS + 1, section, 0)
    out_x[...] = basis[0:wanted]
    out_p[...] = basis[wanted : 2 * wanted]
    out_r[...] = basis[third]
    out_ip[...] = image[wanted : 2 * wanted]


def local(
    n_row, n_col,
    blocks, pattern_rows, pattern_cols, live_count, degree_scale, eigen_block, direction, cutoff,
):
    block_set = blocks[0, 0]
    slots, side, _ = block_set.shape
    wanted, docs = eigen_block.shape
    piece = docs // side
    out_rows = n_col * piece
    row_index = pattern_rows[0, 0]
    slot_id = jnp.arange(slots, dtype=jnp.int32)
    target = jnp.concatenate([row_index, jnp.arange(out_rows, dtype=jnp.int32)])
    bound = jnp.concatenate([slot_id, jnp.full((out_rows,), slots, jnp.int32)])
    before = (
        (target[:, None] == row_index[None, :])
        & (slot_id[None, :] < bound[:, None])
        & (slot_id[None, :] < live_count[0, 0])
    )
    chain = jnp.max(jnp.where(before, slot_id[None, :], -1), axis=1)
    chain = jnp.where(chain < 0, slots, chain)
    tables = jnp.concatenate([pattern_cols[0, 0], chain]).astype(jnp.int32)

    turns = ITERS + 1
    bf16, f32 = jnp.bfloat16, jnp.float32
    sem = pltpu.SemaphoreType.DMA
    vmem = pl.BlockSpec(memory_space=pltpu.VMEM)
    smem = pl.BlockSpec(memory_space=pltpu.SMEM)
    out = jax.ShapeDtypeStruct((wanted, docs), f32)
    return pl.pallas_call(
        functools.partial(body, n_row, n_col, piece, slots, wanted),
        out_shape=(out, out, out, out),
        in_specs=[smem, smem, pl.BlockSpec(memory_space=pl.ANY), vmem, vmem, vmem],
        out_specs=(vmem, vmem, vmem, vmem),
        scratch_shapes=[
            pltpu.VMEM((slots, side, side), bf16),
            pltpu.VMEM((LANES, docs), f32),
            pltpu.VMEM((LANES, docs), f32),
            pltpu.VMEM((n_row * piece, 2 * wanted, side), bf16),
            pltpu.VMEM((slots + 1, 2 * wanted, side), f32),
            pltpu.VMEM((turns, n_row * piece, 2 * wanted, side), bf16),
            pltpu.VMEM((ITERS, n_row * piece, wanted, side), bf16),
            pltpu.VMEM((turns, n_col - 1, piece, 2 * wanted, side), bf16),
            pltpu.VMEM((ITERS, n_col - 1, piece, wanted, side), bf16),
            pltpu.VMEM((turns, n_col - 1, piece, 2 * wanted, side), bf16),
            pltpu.VMEM((ITERS, n_col - 1, piece, wanted, side), bf16),
            pltpu.VMEM((2 * turns, n_col, 2 * wanted, LANES), f32),
            pltpu.VMEM((2 * turns, n_row, 2 * wanted, LANES), f32),
            sem,
            sem((turns, n_row - 1)),
            sem((turns, n_row - 1)),
            sem((ITERS, n_row - 1)),
            sem((ITERS, n_row - 1)),
            sem((turns, n_col - 1)),
            sem((turns, n_col - 1)),
            sem((ITERS, n_col - 1)),
            sem((ITERS, n_col - 1)),
            sem((2 * turns, n_col - 1)),
            sem((2 * turns, n_col - 1)),
            sem((2 * turns, n_row - 1)),
            sem((2 * turns, n_row - 1)),
        ],
        compiler_params=pltpu.CompilerParams(
            collective_id=0, has_side_effects=True, vmem_limit_bytes=56 * 1024 * 1024
        ),
    )(tables, cutoff, block_set, degree_scale[None, :], eigen_block, direction)


def solution(mesh):
    placed = (
        P("brow", "bcol", None, None, None),
        P("brow", "bcol", None),
        P("brow", "bcol", None),
        P("brow", "bcol"),
        P(("brow", "bcol")),
        P(None, ("brow", "bcol")),
        P(None, ("brow", "bcol")),
        P(),
    )
    return jax.shard_map(
        functools.partial(local, mesh.shape["brow"], mesh.shape["bcol"]),
        mesh=mesh,
        in_specs=placed,
        out_specs=(
            P(None, ("brow", "bcol")),
            P(None, ("brow", "bcol")),
            P(None, ("brow", "bcol")),
            P(None, ("brow", "bcol")),
        ),
        check_vma=False,
    )
```

```python
import functools

import jax
import jax.numpy as jnp
from jax import lax
from jax.experimental import pallas as pl
from jax.experimental.pallas import tpu as pltpu
from jax.sharding import PartitionSpec as P

ITERS = 2
NS_STEPS = 8
MESH = pl.DeviceIdType.MESH
LANES = 128


def halves(value):
    high = value.astype(jnp.bfloat16)
    return high, (value - high.astype(jnp.float32)).astype(jnp.bfloat16)


def split_dot(left, right, right_dim):
    rows = left.shape[0]
    left_high, left_low = halves(left)
    right_high, right_low = halves(right)

    def part(first, second):
        return lax.dot_general(
            first,
            second,
            (((1,), (right_dim,)), ((), ())),
            preferred_element_type=jnp.float32,
        )

    main = part(jnp.concatenate([left_high, left_low], 0), right_high)
    return main[:rows] + (main[rows:] + part(left_high, right_low))


def dot(left, right):
    return split_dot(left, right, 0)


def dot_nt(left, right):
    return split_dot(left, right, 1)


def grid_ids(rows):
    shape = (rows, LANES)
    return (
        lax.broadcasted_iota(jnp.int32, shape, 0),
        lax.broadcasted_iota(jnp.int32, shape, 1),
    )


def pad_rows(value, before=0):
    parts = [value, jnp.zeros((LANES - before - value.shape[0], LANES), jnp.float32)]
    if before:
        parts.insert(0, jnp.zeros((before, LANES), jnp.float32))
    return jnp.concatenate(parts, 0)


def inverse_pair(a, b, d):
    scale = 1.0 / (a * d - b * b)
    return d * scale, -(b * scale), a * scale


def inverse_four(m):
    p, q, r = inverse_pair(m[0][0], m[0][1], m[1][1])
    e = [[p * m[0][2 + c] + q * m[1][2 + c] for c in range(2)],
         [q * m[0][2 + c] + r * m[1][2 + c] for c in range(2)]]

    def schur(i, j):
        return m[2 + i][2 + j] - (m[0][2 + i] * e[0][j] + m[1][2 + i] * e[1][j])

    x, y, z = inverse_pair(schur(0, 0), schur(0, 1), schur(1, 1))
    f = [[e[i][0] * x + e[i][1] * y, e[i][0] * y + e[i][1] * z] for i in range(2)]

    def corner(i, j):
        return f[i][0] * e[j][0] + f[i][1] * e[j][1]

    off = q + corner(0, 1)
    return [
        [p + corner(0, 0), off, -f[0][0], -f[0][1]],
        [off, r + corner(1, 1), -f[1][0], -f[1][1]],
        [-f[0][0], -f[1][0], x, y],
        [-f[0][1], -f[1][1], y, z],
    ]


def inverse(matrix):
    side = matrix.shape[0]
    row_id, col_id = grid_ids(side)
    width = 4
    assert side % width == 0

    def sweep(step, now):
        first = step * width
        at_row = [row_id == first + k for k in range(width)]
        at_col = [col_id == first + k for k in range(width)]
        cols = [
            jnp.sum(jnp.where(at_col[k], now, 0.0), axis=1, keepdims=True)
            for k in range(width)
        ]
        rows = [
            jnp.sum(jnp.where(at_row[k], now, 0.0), axis=0, keepdims=True)
            for k in range(width)
        ]
        wide = [jnp.broadcast_to(col, now.shape) for col in cols]
        pivots = [
            [
                jnp.sum(jnp.where(at_row[i], wide[j], 0.0), axis=0, keepdims=True)
                for j in range(width)
            ]
            for i in range(width)
        ]
        inner = inverse_four(pivots)
        scaled_rows = [
            (inner[i][0] * rows[0] + inner[i][1] * rows[1])
            + (inner[i][2] * rows[2] + inner[i][3] * rows[3])
            for i in range(width)
        ]
        out = now - (
            (wide[0] * scaled_rows[0] + wide[1] * scaled_rows[1])
            + (wide[2] * scaled_rows[2] + wide[3] * scaled_rows[3])
        )
        for i in range(width):
            scaled_col = (wide[0] * inner[0][i] + wide[1] * inner[1][i]) + (
                wide[2] * inner[2][i] + wide[3] * inner[3][i]
            )
            out = jnp.where(at_col[i], scaled_col, out)
        for i in range(width):
            line = scaled_rows[i]
            for j in range(width):
                line = jnp.where(at_col[j][0:1], -inner[i][j], line)
            out = jnp.where(at_row[i], line, out)
        return out

    return -lax.fori_loop(0, side // width, sweep, matrix)


def extend_inverse(known, border, offset):
    side = border.shape[0]
    row_id, col_id = grid_ids(side)
    placed = (col_id == row_id + offset).astype(jnp.float32)
    edge = pad_rows(placed - dot(border, known))
    middle = inverse(dot_nt(border, edge))
    return known + dot(edge.T, pad_rows(dot(middle, edge)))


def body(
    n_row, n_col, piece, slots, wanted,
    tables, cutoff, blocks_hbm, scale_ref, eigen_ref, direction_ref,
    out_x, out_p, out_r, out_ip,
    blocks, basis, image, work, sums,
    gather_x, gather_r, part_x, part_r, land_x, land_r, cols_x, rows_x,
    block_sem, gx_send, gx_recv, gr_send, gr_recv, px_send, px_recv, pr_send, pr_recv,
    c_send, c_recv, r_send, r_recv,
):
    me_row, me_col = lax.axis_index("brow"), lax.axis_index("bcol")
    side = blocks.shape[-1]
    block_copy = pltpu.make_async_copy(blocks_hbm, blocks, block_sem)
    block_copy.start()

    def row_peer(step):
        return lax.rem(me_row + step, n_row)

    def col_peer(step):
        return lax.rem(me_col + step, n_col)

    barrier = pltpu.get_barrier_semaphore()
    for step in range(1, n_row):
        pl.semaphore_signal(
            barrier, inc=1, device_id=(row_peer(step), me_col), device_id_type=MESH
        )
    for step in range(1, n_col):
        pl.semaphore_signal(
            barrier, inc=1, device_id=(me_row, col_peer(step)), device_id_type=MESH
        )

    scale = scale_ref[...].reshape(1, piece * side)
    basis[0:wanted] = eigen_ref[...]
    basis[wanted : 2 * wanted] = direction_ref[...]
    basis[2 * wanted :] = jnp.zeros((LANES - 2 * wanted, piece * side), jnp.float32)
    image[...] = jnp.zeros(image.shape, jnp.float32)
    sums[slots] = jnp.zeros(sums.shape[1:], jnp.float32)

    pl.semaphore_wait(barrier, n_row + n_col - 2)
    row_id, col_id = grid_ids(LANES)
    eye = jnp.where((row_id == col_id) & (row_id < 3 * wanted), 1.0, 0.0)

    def remote(src, dst, send, recv, device):
        return pltpu.make_async_remote_copy(
            src_ref=src, dst_ref=dst, send_sem=send, recv_sem=recv,
            device_id=device, device_id_type=MESH,
        )

    def spot(p):
        return slice(p * side, (p + 1) * side)

    def apply_graph(turn, first, count, gather, part, land, sems, meanwhile):
        g_send, g_recv, p_send, p_recv = sems
        rows = slice(first, first + count)
        mine = pl.ds(me_row * piece, piece)
        for p in range(piece):
            gather[turn, me_row * piece + p] = (
                scale[:, spot(p)] * basis[rows, spot(p)]
            ).astype(jnp.bfloat16)
        copies = []
        for step in range(1, n_row):
            copies.append(
                remote(
                    gather.at[turn, mine], gather.at[turn, mine],
                    g_send.at[turn, step - 1], g_recv.at[turn, step - 1],
                    (row_peer(step), me_col),
                )
            )
            copies[-1].start()
        found = meanwhile()
        for copy in copies:
            copy.wait()

        def move(k, carry):
            work[k, 0:count] = gather[turn, k]
            return carry

        lax.fori_loop(0, n_row * piece, move, 0)

        def slot(s, carry):
            product = lax.dot_general(
                work[tables[s], 0:count],
                blocks[s],
                (((1,), (1,)), ((), ())),
                preferred_element_type=jnp.float32,
            )
            sums[s, 0:count] = product + sums[tables[slots + s], 0:count]
            return carry

        lax.fori_loop(0, slots, slot, 0, unroll=4)

        def row_sum(owner, p):
            return sums[tables[2 * slots + owner * piece + p], 0:count]

        copies = []
        for step in range(1, n_col):
            owner = col_peer(step)
            for p in range(piece):
                part[turn, step - 1, p] = row_sum(owner, p).astype(jnp.bfloat16)
            copies.append(
                remote(
                    part.at[turn, step - 1], land.at[turn, step - 1],
                    p_send.at[turn, step - 1], p_recv.at[turn, step - 1],
                    (me_row, owner),
                )
            )
            copies[-1].start()
        for copy in copies:
            copy.wait()
        for p in range(piece):
            total = row_sum(me_col, p)
            for step in range(1, n_col):
                total = total + land[turn, step - 1, p].astype(jnp.float32)
            image[rows, spot(p)] = basis[rows, spot(p)] - scale[:, spot(p)] * total
        return found

    def add_up(turn, value):
        for land, send, recv, count, me in (
            (cols_x, c_send, c_recv, n_col, me_col),
            (rows_x, r_send, r_recv, n_row, me_row),
        ):
            land[turn, me] = value
            copies = []
            for step in range(1, count):
                device = (
                    (me_row, col_peer(step)) if land is cols_x else (row_peer(step), me_col)
                )
                copies.append(
                    remote(
                        land.at[turn, me], land.at[turn, me],
                        send.at[turn, step - 1], recv.at[turn, step - 1], device,
                    )
                )
                copies[-1].start()
            for copy in copies:
                copy.wait()
            value = land[turn, 0]
            for k in range(1, count):
                value = value + land[turn, k]
        return value

    pair = slice(0, 2 * wanted)
    third = slice(2 * wanted, 3 * wanted)
    x_sems = (gx_send, gx_recv, px_send, px_recv)
    r_sems = (gr_send, gr_recv, pr_send, pr_recv)

    def section(turn, carry):
        def wait_blocks():
            @pl.when(turn == 0)
            def _():
                block_copy.wait()

        apply_graph(turn, 0, 2 * wanted, gather_x, part_x, land_x, x_sems, wait_blocks)
        both = jnp.concatenate([basis[pair], image[pair]], 0)
        grams = add_up(2 * turn, dot_nt(basis[pair], both))
        flipped = pad_rows(grams).T
        narrow = grid_ids(wanted)[1] < wanted
        gram_inv = pad_rows(inverse(jnp.where(narrow, grams[0:wanted], 0.0)))
        rayleigh_t = jnp.where(narrow, flipped[2 * wanted : 3 * wanted], 0.0)
        quotient_t = dot(rayleigh_t, gram_inv)
        basis[third] = image[0:wanted] - dot(quotient_t, basis[...])

        @pl.when(turn < ITERS)
        def _():
            def pair_algebra():
                half = grid_ids(wanted)[1] < 2 * wanted
                cross_t = pad_rows(flipped[2 * wanted :])
                return cross_t + cross_t.T, extend_inverse(
                    gram_inv, jnp.where(half, grams[wanted : 2 * wanted], 0.0), wanted
                )

            cross_twice, pair_inv = apply_graph(
                turn, 2 * wanted, wanted, gather_r, part_r, land_r, r_sems, pair_algebra
            )
            residual = basis[third]
            border = add_up(
                2 * turn + 1,
                jnp.concatenate(
                    [
                        dot_nt(residual, basis[...]),
                        0.5
                        * (dot_nt(image[third], basis[...]) + dot_nt(residual, image[...])),
                    ],
                    0,
                ),
            )
            full_inv = extend_inverse(pair_inv, border[0:wanted], 2 * wanted)
            low = pad_rows(border[wanted:], 2 * wanted)
            gram_a = (
                0.5 * cross_twice
                + low
                + jnp.where(row_id < 2 * wanted, low.T, 0.0)
            )
            shifted = cutoff[0] * eye - dot(gram_a, full_inv)
            square = dot(shifted, shifted)
            trace = jnp.sum(
                jnp.sum(jnp.where(row_id == col_id, square, 0.0), axis=1, keepdims=True),
                axis=0,
                keepdims=True,
            )
            norm = 1.0 / jnp.sqrt(trace + 1e-06)
            sign = (1.5 * norm) * shifted - (0.5 * norm) * dot(
                shifted * norm, square * norm
            )

            def newton(_, now):
                return 1.5 * now - 0.5 * dot(now, dot(now, now))

            sign = lax.fori_loop(0, NS_STEPS - 1, newton, sign)
            coeffs = 0.5 * (eye + sign)[0:wanted]
            mixed = jnp.concatenate([coeffs, jnp.where(narrow, 0.0, coeffs)], 0)
            basis[pair] = dot(mixed, basis[...])

        return carry

    lax.fori_loop(0, ITERS + 1, section, 0)
    out_x[...] = basis[0:wanted]
    out_p[...] = basis[wanted : 2 * wanted]
    out_r[...] = basis[third]
    out_ip[...] = image[wanted : 2 * wanted]


def hand_on(*refs):
    for source, target in zip(refs[:4], refs[4:]):
        target[...] = source[...]


def local(
    n_row, n_col,
    blocks, pattern_rows, pattern_cols, live_count, degree_scale, eigen_block, direction, cutoff,
):
    block_set = blocks[0, 0]
    slots, side, _ = block_set.shape
    wanted, docs = eigen_block.shape
    piece = docs // side
    out_rows = n_col * piece
    row_index = pattern_rows[0, 0]
    slot_id = jnp.arange(slots, dtype=jnp.int32)
    target = jnp.concatenate([row_index, jnp.arange(out_rows, dtype=jnp.int32)])
    bound = jnp.concatenate([slot_id, jnp.full((out_rows,), slots, jnp.int32)])
    before = (
        (target[:, None] == row_index[None, :])
        & (slot_id[None, :] < bound[:, None])
        & (slot_id[None, :] < live_count[0, 0])
    )
    chain = jnp.max(jnp.where(before, slot_id[None, :], -1), axis=1)
    chain = jnp.where(chain < 0, slots, chain)
    tables = jnp.concatenate([pattern_cols[0, 0], chain]).astype(jnp.int32)

    turns = ITERS + 1
    bf16, f32 = jnp.bfloat16, jnp.float32
    sem = pltpu.SemaphoreType.DMA
    vmem = pl.BlockSpec(memory_space=pltpu.VMEM)
    smem = pl.BlockSpec(memory_space=pltpu.SMEM)
    out = jax.ShapeDtypeStruct((wanted, docs), f32)
    results = pl.pallas_call(
        functools.partial(body, n_row, n_col, piece, slots, wanted),
        out_shape=(out, out, out, out),
        in_specs=[smem, smem, pl.BlockSpec(memory_space=pl.ANY), vmem, vmem, vmem],
        out_specs=(vmem, vmem, vmem, vmem),
        scratch_shapes=[
            pltpu.VMEM((slots, side, side), bf16),
            pltpu.VMEM((LANES, docs), f32),
            pltpu.VMEM((LANES, docs), f32),
            pltpu.VMEM((n_row * piece, 2 * wanted, side), bf16),
            pltpu.VMEM((slots + 1, 2 * wanted, side), f32),
            pltpu.VMEM((turns, n_row * piece, 2 * wanted, side), bf16),
            pltpu.VMEM((ITERS, n_row * piece, wanted, side), bf16),
            pltpu.VMEM((turns, n_col - 1, piece, 2 * wanted, side), bf16),
            pltpu.VMEM((ITERS, n_col - 1, piece, wanted, side), bf16),
            pltpu.VMEM((turns, n_col - 1, piece, 2 * wanted, side), bf16),
            pltpu.VMEM((ITERS, n_col - 1, piece, wanted, side), bf16),
            pltpu.VMEM((2 * turns, n_col, 2 * wanted, LANES), f32),
            pltpu.VMEM((2 * turns, n_row, 2 * wanted, LANES), f32),
            sem,
            sem((turns, n_row - 1)),
            sem((turns, n_row - 1)),
            sem((ITERS, n_row - 1)),
            sem((ITERS, n_row - 1)),
            sem((turns, n_col - 1)),
            sem((turns, n_col - 1)),
            sem((ITERS, n_col - 1)),
            sem((ITERS, n_col - 1)),
            sem((2 * turns, n_col - 1)),
            sem((2 * turns, n_col - 1)),
            sem((2 * turns, n_row - 1)),
            sem((2 * turns, n_row - 1)),
        ],
        compiler_params=pltpu.CompilerParams(
            collective_id=0, has_side_effects=True, vmem_limit_bytes=56 * 1024 * 1024
        ),
    )(tables, cutoff, block_set, degree_scale, eigen_block, direction)
    return pl.pallas_call(
        hand_on,
        out_shape=(out, out, out, out),
        in_specs=[vmem] * 4,
        out_specs=(vmem, vmem, vmem, vmem),
    )(*results)


def solution(mesh):
    placed = (
        P("brow", "bcol", None, None, None),
        P("brow", "bcol", None),
        P("brow", "bcol", None),
        P("brow", "bcol"),
        P(("brow", "bcol")),
        P(None, ("brow", "bcol")),
        P(None, ("brow", "bcol")),
        P(),
    )
    return jax.shard_map(
        functools.partial(local, mesh.shape["brow"], mesh.shape["bcol"]),
        mesh=mesh,
        in_specs=placed,
        out_specs=(
            P(None, ("brow", "bcol")),
            P(None, ("brow", "bcol")),
            P(None, ("brow", "bcol")),
            P(None, ("brow", "bcol")),
        ),
        check_vma=False,
    )
```

```python
import functools

import jax
import jax.numpy as jnp
from jax import lax
from jax.experimental import pallas as pl
from jax.experimental.pallas import tpu as pltpu
from jax.sharding import PartitionSpec as P

ITERS = 2
NS_STEPS = 8
MESH = pl.DeviceIdType.MESH
LANES = 128


def halves(value):
    high = value.astype(jnp.bfloat16)
    return high, (value - high.astype(jnp.float32)).astype(jnp.bfloat16)


def split_dot(left, right, right_dim):
    rows = left.shape[0]
    left_high, left_low = halves(left)
    right_high, right_low = halves(right)

    def part(first, second):
        return lax.dot_general(
            first,
            second,
            (((1,), (right_dim,)), ((), ())),
            preferred_element_type=jnp.float32,
        )

    main = part(jnp.concatenate([left_high, left_low], 0), right_high)
    return main[:rows] + (main[rows:] + part(left_high, right_low))


def dot(left, right):
    return split_dot(left, right, 0)


def dot_nt(left, right):
    return split_dot(left, right, 1)


def grid_ids(rows):
    shape = (rows, LANES)
    return (
        lax.broadcasted_iota(jnp.int32, shape, 0),
        lax.broadcasted_iota(jnp.int32, shape, 1),
    )


def pad_rows(value, before=0):
    parts = [value, jnp.zeros((LANES - before - value.shape[0], LANES), jnp.float32)]
    if before:
        parts.insert(0, jnp.zeros((before, LANES), jnp.float32))
    return jnp.concatenate(parts, 0)


def inverse_pair(a, b, d):
    scale = 1.0 / (a * d - b * b)
    return d * scale, -(b * scale), a * scale


def inverse_four(m):
    p, q, r = inverse_pair(m[0][0], m[0][1], m[1][1])
    e = [[p * m[0][2 + c] + q * m[1][2 + c] for c in range(2)],
         [q * m[0][2 + c] + r * m[1][2 + c] for c in range(2)]]

    def schur(i, j):
        return m[2 + i][2 + j] - (m[0][2 + i] * e[0][j] + m[1][2 + i] * e[1][j])

    x, y, z = inverse_pair(schur(0, 0), schur(0, 1), schur(1, 1))
    f = [[e[i][0] * x + e[i][1] * y, e[i][0] * y + e[i][1] * z] for i in range(2)]

    def corner(i, j):
        return f[i][0] * e[j][0] + f[i][1] * e[j][1]

    off = q + corner(0, 1)
    return [
        [p + corner(0, 0), off, -f[0][0], -f[0][1]],
        [off, r + corner(1, 1), -f[1][0], -f[1][1]],
        [-f[0][0], -f[1][0], x, y],
        [-f[0][1], -f[1][1], y, z],
    ]


def inverse(matrix):
    side = matrix.shape[0]
    row_id, col_id = grid_ids(side)
    width = 4
    assert side % width == 0

    def sweep(step, now):
        first = step * width
        at_row = [row_id == first + k for k in range(width)]
        at_col = [col_id == first + k for k in range(width)]
        cols = [
            jnp.sum(jnp.where(at_col[k], now, 0.0), axis=1, keepdims=True)
            for k in range(width)
        ]
        rows = [
            jnp.sum(jnp.where(at_row[k], now, 0.0), axis=0, keepdims=True)
            for k in range(width)
        ]
        wide = [jnp.broadcast_to(col, now.shape) for col in cols]
        pivots = [
            [
                jnp.sum(jnp.where(at_row[i], wide[j], 0.0), axis=0, keepdims=True)
                for j in range(width)
            ]
            for i in range(width)
        ]
        inner = inverse_four(pivots)
        scaled_rows = [
            (inner[i][0] * rows[0] + inner[i][1] * rows[1])
            + (inner[i][2] * rows[2] + inner[i][3] * rows[3])
            for i in range(width)
        ]
        out = now - (
            (wide[0] * scaled_rows[0] + wide[1] * scaled_rows[1])
            + (wide[2] * scaled_rows[2] + wide[3] * scaled_rows[3])
        )
        for i in range(width):
            scaled_col = (wide[0] * inner[0][i] + wide[1] * inner[1][i]) + (
                wide[2] * inner[2][i] + wide[3] * inner[3][i]
            )
            out = jnp.where(at_col[i], scaled_col, out)
        for i in range(width):
            line = scaled_rows[i]
            for j in range(width):
                line = jnp.where(at_col[j][0:1], -inner[i][j], line)
            out = jnp.where(at_row[i], line, out)
        return out

    return -lax.fori_loop(0, side // width, sweep, matrix)


def extend_inverse(known, border, offset):
    side = border.shape[0]
    row_id, col_id = grid_ids(side)
    placed = (col_id == row_id + offset).astype(jnp.float32)
    edge = pad_rows(placed - dot(border, known))
    middle = inverse(dot_nt(border, edge))
    return known + dot(edge.T, pad_rows(dot(middle, edge)))


def body(
    n_row, n_col, piece, slots, wanted,
    tables, cutoff, blocks_hbm, scale_ref, eigen_ref, direction_ref,
    out_x, out_p, out_r, out_ip,
    blocks, basis, image, work, sums,
    gather_x, gather_r, part_x, part_r, land_x, land_r,
    own_x, cols_x, rows_x, all_x, gram_ref, cross_ref,
    block_sem, gx_send, gx_recv, gr_send, gr_recv, px_send, px_recv, pr_send, pr_recv,
    c_send, c_recv, r_send, r_recv, a_send, a_recv,
):
    me_row, me_col = lax.axis_index("brow"), lax.axis_index("bcol")
    side = blocks.shape[-1]
    block_copy = pltpu.make_async_copy(blocks_hbm, blocks, block_sem)
    block_copy.start()

    def row_peer(step):
        return lax.rem(me_row + step, n_row)

    def col_peer(step):
        return lax.rem(me_col + step, n_col)

    barrier = pltpu.get_barrier_semaphore()
    for step in range(1, n_row):
        pl.semaphore_signal(
            barrier, inc=1, device_id=(row_peer(step), me_col), device_id_type=MESH
        )
    for step in range(1, n_col):
        pl.semaphore_signal(
            barrier, inc=1, device_id=(me_row, col_peer(step)), device_id_type=MESH
        )

    scale = scale_ref[...].reshape(1, piece * side)
    basis[0:wanted] = eigen_ref[...]
    basis[wanted : 2 * wanted] = direction_ref[...]
    basis[2 * wanted :] = jnp.zeros((LANES - 2 * wanted, piece * side), jnp.float32)
    image[...] = jnp.zeros(image.shape, jnp.float32)
    sums[slots] = jnp.zeros(sums.shape[1:], jnp.float32)

    pl.semaphore_wait(barrier, n_row + n_col - 2)
    row_id, col_id = grid_ids(LANES)
    eye = jnp.where((row_id == col_id) & (row_id < 3 * wanted), 1.0, 0.0)

    def remote(src, dst, send, recv, device):
        return pltpu.make_async_remote_copy(
            src_ref=src, dst_ref=dst, send_sem=send, recv_sem=recv,
            device_id=device, device_id_type=MESH,
        )

    def spot(p):
        return slice(p * side, (p + 1) * side)

    def apply_graph(turn, first, count, gather, part, land, sems, meanwhile):
        g_send, g_recv, p_send, p_recv = sems
        rows = slice(first, first + count)
        mine = pl.ds(me_row * piece, piece)
        for p in range(piece):
            gather[turn, me_row * piece + p] = (
                scale[:, spot(p)] * basis[rows, spot(p)]
            ).astype(jnp.bfloat16)
        copies = []
        for step in range(1, n_row):
            copies.append(
                remote(
                    gather.at[turn, mine], gather.at[turn, mine],
                    g_send.at[turn, step - 1], g_recv.at[turn, step - 1],
                    (row_peer(step), me_col),
                )
            )
            copies[-1].start()
        found = meanwhile()
        for copy in copies:
            copy.wait()

        def move(k, carry):
            work[k, 0:count] = gather[turn, k]
            return carry

        lax.fori_loop(0, n_row * piece, move, 0)

        def slot(s, carry):
            product = lax.dot_general(
                work[tables[s], 0:count],
                blocks[s],
                (((1,), (1,)), ((), ())),
                preferred_element_type=jnp.float32,
            )
            sums[s, 0:count] = product + sums[tables[slots + s], 0:count]
            return carry

        lax.fori_loop(0, slots, slot, 0, unroll=4)

        def row_sum(owner, p):
            return sums[tables[2 * slots + owner * piece + p], 0:count]

        copies = []
        for step in range(1, n_col):
            owner = col_peer(step)
            for p in range(piece):
                part[turn, step - 1, p] = row_sum(owner, p).astype(jnp.bfloat16)
            copies.append(
                remote(
                    part.at[turn, step - 1], land.at[turn, step - 1],
                    p_send.at[turn, step - 1], p_recv.at[turn, step - 1],
                    (me_row, owner),
                )
            )
            copies[-1].start()
        for copy in copies:
            copy.wait()
        for p in range(piece):
            total = row_sum(me_col, p)
            for step in range(1, n_col):
                total = total + land[turn, step - 1, p].astype(jnp.float32)
            image[rows, spot(p)] = basis[rows, spot(p)] - scale[:, spot(p)] * total
        return found

    def swap(turn, land, send, recv, along_col, source):
        me = me_col if along_col else me_row
        copies = []
        for step in range(1, n_col if along_col else n_row):
            peer = col_peer(step) if along_col else row_peer(step)
            device = (me_row, peer) if along_col else (peer, me_col)
            copies.append(
                remote(
                    source(peer), land.at[turn, me],
                    send.at[turn, step - 1], recv.at[turn, step - 1], device,
                )
            )
            copies[-1].start()
        for copy in copies:
            copy.wait()

    def total_of(land, turn, count):
        value = land[turn, 0]
        for k in range(1, count):
            value = value + land[turn, k]
        return value

    def add_up(turn, value):
        height = LANES // n_col
        for k in range(n_col):
            own_x[turn, k] = value[k * height : (k + 1) * height]
        cols_x[turn, me_col] = own_x[turn, me_col]
        swap(turn, cols_x, c_send, c_recv, True, lambda peer: own_x.at[turn, peer])
        rows_x[turn, me_row] = total_of(cols_x, turn, n_col)
        swap(turn, rows_x, r_send, r_recv, False, lambda peer: rows_x.at[turn, me_row])
        all_x[turn, me_col] = total_of(rows_x, turn, n_row)
        swap(turn, all_x, a_send, a_recv, True, lambda peer: all_x.at[turn, me_col])
        return jnp.concatenate([all_x[turn, k] for k in range(n_col)], 0)

    pair = slice(0, 2 * wanted)
    third = slice(2 * wanted, 3 * wanted)
    x_sems = (gx_send, gx_recv, px_send, px_recv)
    r_sems = (gr_send, gr_recv, pr_send, pr_recv)

    apply_graph(0, 0, 2 * wanted, gather_x, part_x, land_x, x_sems, block_copy.wait)
    both = jnp.concatenate([basis[pair], image[pair]], 0)
    grams = add_up(ITERS, pad_rows(dot_nt(basis[pair], both)))
    gram_ref[...] = jnp.where(col_id < 2 * wanted, grams, 0.0)
    cross_ref[...] = pad_rows(grams.T[2 * wanted :]).T

    def section(turn, carry):
        narrow = grid_ids(wanted)[1] < wanted
        half = grid_ids(wanted)[1] < 2 * wanted
        gram_pair = gram_ref[...]
        cross_pair = cross_ref[...]
        gram_inv = pad_rows(inverse(jnp.where(narrow, gram_pair[0:wanted], 0.0)))
        rayleigh_t = jnp.where(narrow, cross_pair.T[0:wanted], 0.0)
        quotient_t = dot(rayleigh_t, gram_inv)
        basis[third] = image[0:wanted] - dot(quotient_t, basis[...])

        @pl.when(turn < ITERS)
        def _():
            def pair_algebra():
                return extend_inverse(
                    gram_inv, jnp.where(half, gram_pair[wanted : 2 * wanted], 0.0), wanted
                )

            pair_inv = apply_graph(
                turn, 2 * wanted, wanted, gather_r, part_r, land_r, r_sems, pair_algebra
            )
            everything = jnp.concatenate([basis[...], image[...]], 0)
            by_residual = dot_nt(basis[third], everything)
            border = add_up(
                turn,
                pad_rows(
                    jnp.concatenate(
                        [
                            by_residual[:, :LANES],
                            by_residual[:, LANES:],
                            dot_nt(image[third], basis[...]),
                        ],
                        0,
                    )
                ),
            )

            def around(rows, cols):
                low = pad_rows(rows, 2 * wanted)
                right = pad_rows(cols, 2 * wanted).T
                return low + jnp.where(row_id < 2 * wanted, right, 0.0)

            full_inv = extend_inverse(pair_inv, border[0:wanted], 2 * wanted)
            gram_b = gram_pair + around(border[0:wanted], border[0:wanted])
            cross = cross_pair + around(border[wanted : 2 * wanted], border[third])
            gram_a = 0.5 * (cross + cross.T)
            shifted = cutoff[0] * eye - dot(gram_a, full_inv)
            square = dot(shifted, shifted)
            trace = jnp.sum(
                jnp.sum(jnp.where(row_id == col_id, square, 0.0), axis=1, keepdims=True),
                axis=0,
                keepdims=True,
            )
            norm = 1.0 / jnp.sqrt(trace + 1e-06)
            sign = (1.5 * norm) * shifted - (0.5 * norm) * dot(
                shifted * norm, square * norm
            )

            def newton(_, now):
                return 1.5 * now - 0.5 * dot(now, dot(now, now))

            sign = lax.fori_loop(0, NS_STEPS - 1, newton, sign)
            coeffs = 0.5 * (eye + sign)[0:wanted]
            mixed = jnp.concatenate([coeffs, jnp.where(narrow, 0.0, coeffs)], 0)
            basis[pair] = dot(mixed, basis[...])
            image[pair] = dot(mixed, image[...])
            square_mix = pad_rows(mixed)
            gram_ref[...] = dot_nt(dot(square_mix, gram_b), square_mix)
            cross_ref[...] = dot_nt(dot(square_mix, cross), square_mix)

        return carry

    lax.fori_loop(0, ITERS + 1, section, 0)
    out_x[...] = basis[0:wanted]
    out_p[...] = basis[wanted : 2 * wanted]
    out_r[...] = basis[third]
    out_ip[...] = image[wanted : 2 * wanted]


def hand_on(*refs):
    for source, target in zip(refs[:4], refs[4:]):
        target[...] = source[...]


def local(
    n_row, n_col,
    blocks, pattern_rows, pattern_cols, live_count, degree_scale, eigen_block, direction, cutoff,
):
    block_set = blocks[0, 0]
    slots, side, _ = block_set.shape
    wanted, docs = eigen_block.shape
    piece = docs // side
    out_rows = n_col * piece
    row_index = pattern_rows[0, 0]
    slot_id = jnp.arange(slots, dtype=jnp.int32)
    target = jnp.concatenate([row_index, jnp.arange(out_rows, dtype=jnp.int32)])
    bound = jnp.concatenate([slot_id, jnp.full((out_rows,), slots, jnp.int32)])
    before = (
        (target[:, None] == row_index[None, :])
        & (slot_id[None, :] < bound[:, None])
        & (slot_id[None, :] < live_count[0, 0])
    )
    chain = jnp.max(jnp.where(before, slot_id[None, :], -1), axis=1)
    chain = jnp.where(chain < 0, slots, chain)
    tables = jnp.concatenate([pattern_cols[0, 0], chain]).astype(jnp.int32)

    turns = ITERS + 1
    bf16, f32 = jnp.bfloat16, jnp.float32
    sem = pltpu.SemaphoreType.DMA
    vmem = pl.BlockSpec(memory_space=pltpu.VMEM)
    smem = pl.BlockSpec(memory_space=pltpu.SMEM)
    out = jax.ShapeDtypeStruct((wanted, docs), f32)
    results = pl.pallas_call(
        functools.partial(body, n_row, n_col, piece, slots, wanted),
        out_shape=(out, out, out, out),
        in_specs=[smem, smem, pl.BlockSpec(memory_space=pl.ANY), vmem, vmem, vmem],
        out_specs=(vmem, vmem, vmem, vmem),
        scratch_shapes=[
            pltpu.VMEM((slots, side, side), bf16),
            pltpu.VMEM((LANES, docs), f32),
            pltpu.VMEM((LANES, docs), f32),
            pltpu.VMEM((n_row * piece, 2 * wanted, side), bf16),
            pltpu.VMEM((slots + 1, 2 * wanted, side), f32),
            pltpu.VMEM((1, n_row * piece, 2 * wanted, side), bf16),
            pltpu.VMEM((ITERS, n_row * piece, wanted, side), bf16),
            pltpu.VMEM((1, n_col - 1, piece, 2 * wanted, side), bf16),
            pltpu.VMEM((ITERS, n_col - 1, piece, wanted, side), bf16),
            pltpu.VMEM((1, n_col - 1, piece, 2 * wanted, side), bf16),
            pltpu.VMEM((ITERS, n_col - 1, piece, wanted, side), bf16),
            pltpu.VMEM((turns, n_col, LANES // n_col, LANES), f32),
            pltpu.VMEM((turns, n_col, LANES // n_col, LANES), f32),
            pltpu.VMEM((turns, n_row, LANES // n_col, LANES), f32),
            pltpu.VMEM((turns, n_col, LANES // n_col, LANES), f32),
            pltpu.VMEM((LANES, LANES), f32),
            pltpu.VMEM((LANES, LANES), f32),
            sem,
            sem((1, n_row - 1)),
            sem((1, n_row - 1)),
            sem((ITERS, n_row - 1)),
            sem((ITERS, n_row - 1)),
            sem((1, n_col - 1)),
            sem((1, n_col - 1)),
            sem((ITERS, n_col - 1)),
            sem((ITERS, n_col - 1)),
            sem((turns, n_col - 1)),
            sem((turns, n_col - 1)),
            sem((turns, n_row - 1)),
            sem((turns, n_row - 1)),
            sem((turns, n_col - 1)),
            sem((turns, n_col - 1)),
        ],
        compiler_params=pltpu.CompilerParams(
            collective_id=0, has_side_effects=True, vmem_limit_bytes=56 * 1024 * 1024
        ),
    )(tables, cutoff, block_set, degree_scale, eigen_block, direction)
    return pl.pallas_call(
        hand_on,
        out_shape=(out, out, out, out),
        in_specs=[vmem] * 4,
        out_specs=(vmem, vmem, vmem, vmem),
    )(*results)


def solution(mesh):
    placed = (
        P("brow", "bcol", None, None, None),
        P("brow", "bcol", None),
        P("brow", "bcol", None),
        P("brow", "bcol"),
        P(("brow", "bcol")),
        P(None, ("brow", "bcol")),
        P(None, ("brow", "bcol")),
        P(),
    )
    return jax.shard_map(
        functools.partial(local, mesh.shape["brow"], mesh.shape["bcol"]),
        mesh=mesh,
        in_specs=placed,
        out_specs=(
            P(None, ("brow", "bcol")),
            P(None, ("brow", "bcol")),
            P(None, ("brow", "bcol")),
            P(None, ("brow", "bcol")),
        ),
        check_vma=False,
    )
```

```python
import functools

import jax
import jax.numpy as jnp
from jax import lax
from jax.experimental import pallas as pl
from jax.experimental.pallas import tpu as pltpu
from jax.sharding import PartitionSpec as P

ITERS = 2
NS_STEPS = 8
MESH = pl.DeviceIdType.MESH
LANES = 128


def halves(value):
    high = value.astype(jnp.bfloat16)
    return high, (value - high.astype(jnp.float32)).astype(jnp.bfloat16)


def split_dot(left, right, right_dim):
    rows = left.shape[0]
    left_high, left_low = halves(left)
    right_high, right_low = halves(right)

    def part(first, second):
        return lax.dot_general(
            first,
            second,
            (((1,), (right_dim,)), ((), ())),
            preferred_element_type=jnp.float32,
        )

    main = part(jnp.concatenate([left_high, left_low], 0), right_high)
    return main[:rows] + (main[rows:] + part(left_high, right_low))


def dot(left, right):
    return split_dot(left, right, 0)


def dot_nt(left, right):
    return split_dot(left, right, 1)


def grid_ids(rows):
    shape = (rows, LANES)
    return (
        lax.broadcasted_iota(jnp.int32, shape, 0),
        lax.broadcasted_iota(jnp.int32, shape, 1),
    )


def pad_rows(value, before=0):
    parts = [value, jnp.zeros((LANES - before - value.shape[0], LANES), jnp.float32)]
    if before:
        parts.insert(0, jnp.zeros((before, LANES), jnp.float32))
    return jnp.concatenate(parts, 0)


def inverse_pair(a, b, d):
    scale = 1.0 / (a * d - b * b)
    return d * scale, -(b * scale), a * scale


def inverse_four(m):
    p, q, r = inverse_pair(m[0][0], m[0][1], m[1][1])
    e = [[p * m[0][2 + c] + q * m[1][2 + c] for c in range(2)],
         [q * m[0][2 + c] + r * m[1][2 + c] for c in range(2)]]

    def schur(i, j):
        return m[2 + i][2 + j] - (m[0][2 + i] * e[0][j] + m[1][2 + i] * e[1][j])

    x, y, z = inverse_pair(schur(0, 0), schur(0, 1), schur(1, 1))
    f = [[e[i][0] * x + e[i][1] * y, e[i][0] * y + e[i][1] * z] for i in range(2)]

    def corner(i, j):
        return f[i][0] * e[j][0] + f[i][1] * e[j][1]

    off = q + corner(0, 1)
    return [
        [p + corner(0, 0), off, -f[0][0], -f[0][1]],
        [off, r + corner(1, 1), -f[1][0], -f[1][1]],
        [-f[0][0], -f[1][0], x, y],
        [-f[0][1], -f[1][1], y, z],
    ]


def inverse(matrix):
    side = matrix.shape[0]
    row_id, col_id = grid_ids(side)
    width = 4
    assert side % width == 0

    def sweep(step, now):
        first = step * width
        at_row = [row_id == first + k for k in range(width)]
        at_col = [col_id == first + k for k in range(width)]
        cols = [
            jnp.sum(jnp.where(at_col[k], now, 0.0), axis=1, keepdims=True)
            for k in range(width)
        ]
        rows = [
            jnp.sum(jnp.where(at_row[k], now, 0.0), axis=0, keepdims=True)
            for k in range(width)
        ]
        wide = [jnp.broadcast_to(col, now.shape) for col in cols]
        pivots = [
            [
                jnp.sum(jnp.where(at_row[i], wide[j], 0.0), axis=0, keepdims=True)
                for j in range(width)
            ]
            for i in range(width)
        ]
        inner = inverse_four(pivots)
        scaled_rows = [
            (inner[i][0] * rows[0] + inner[i][1] * rows[1])
            + (inner[i][2] * rows[2] + inner[i][3] * rows[3])
            for i in range(width)
        ]
        out = now - (
            (wide[0] * scaled_rows[0] + wide[1] * scaled_rows[1])
            + (wide[2] * scaled_rows[2] + wide[3] * scaled_rows[3])
        )
        for i in range(width):
            scaled_col = (wide[0] * inner[0][i] + wide[1] * inner[1][i]) + (
                wide[2] * inner[2][i] + wide[3] * inner[3][i]
            )
            out = jnp.where(at_col[i], scaled_col, out)
        for i in range(width):
            line = scaled_rows[i]
            for j in range(width):
                line = jnp.where(at_col[j][0:1], -inner[i][j], line)
            out = jnp.where(at_row[i], line, out)
        return out

    return -lax.fori_loop(0, side // width, sweep, matrix)


def extend_inverse(known, border, offset):
    side = border.shape[0]
    row_id, col_id = grid_ids(side)
    placed = (col_id == row_id + offset).astype(jnp.float32)
    edge = pad_rows(placed - dot(border, known))
    middle = inverse(dot_nt(border, edge))
    return known + dot(edge.T, pad_rows(dot(middle, edge)))


def body(
    n_row, n_col, piece, slots, wanted,
    col_table, prev_table, last_table, cutoff, blocks_hbm, scale_ref, eigen_ref, direction_ref,
    out_x, out_p, out_r, out_ip,
    blocks, basis, image, moved, work, sums, gather, part, land, kept,
    own_x, cols_x, rows_x, all_x, pair_cols, pair_rows, gram_ref, cross_ref,
    block_sem, g_send, g_recv, p_send, p_recv,
    c_send, c_recv, r_send, r_recv, a_send, a_recv, d_send, d_recv, e_send, e_recv,
):
    me_row, me_col = lax.axis_index("brow"), lax.axis_index("bcol")
    side = blocks.shape[-1]
    block_copy = pltpu.make_async_copy(blocks_hbm, blocks, block_sem)
    block_copy.start()

    def row_peer(step):
        return lax.rem(me_row + step, n_row)

    def col_peer(step):
        return lax.rem(me_col + step, n_col)

    barrier = pltpu.get_barrier_semaphore()
    for step in range(1, n_row):
        pl.semaphore_signal(
            barrier, inc=1, device_id=(row_peer(step), me_col), device_id_type=MESH
        )
    for step in range(1, n_col):
        pl.semaphore_signal(
            barrier, inc=1, device_id=(me_row, col_peer(step)), device_id_type=MESH
        )

    scale = scale_ref[...].reshape(1, piece * side)
    basis[0:wanted] = eigen_ref[...]
    basis[wanted : 2 * wanted] = direction_ref[...]
    basis[2 * wanted :] = jnp.zeros((LANES - 2 * wanted, piece * side), jnp.float32)
    image[...] = jnp.zeros(image.shape, jnp.float32)
    sums[slots] = jnp.zeros(sums.shape[1:], jnp.float32)

    pl.semaphore_wait(barrier, n_row + n_col - 2)
    row_id, col_id = grid_ids(LANES)
    eye = jnp.where((row_id == col_id) & (row_id < 3 * wanted), 1.0, 0.0)

    def remote(src, dst, send, recv, device):
        return pltpu.make_async_remote_copy(
            src_ref=src, dst_ref=dst, send_sem=send, recv_sem=recv,
            device_id=device, device_id_type=MESH,
        )

    def spot(p):
        return slice(p * side, (p + 1) * side)

    def gather_copies(phase):
        mine = pl.ds(me_row * piece, piece)
        return [
            remote(
                gather.at[phase, mine], gather.at[phase, mine],
                g_send.at[phase, step - 1], g_recv.at[phase, step - 1],
                (row_peer(step), me_col),
            )
            for step in range(1, n_row)
        ]

    def start_gather(phase, panel, first):
        for p in range(piece):
            gather[phase, me_row * piece + p] = (
                scale[:, spot(p)] * panel[first : first + wanted, spot(p)]
            ).astype(jnp.bfloat16)
        for copy in gather_copies(phase):
            copy.start()

    def finish_gather(phase):
        for copy in gather_copies(phase):
            copy.wait()

        def move(k, carry):
            work[k] = gather[phase, k]
            return carry

        lax.fori_loop(0, n_row * piece, move, 0, unroll=4)

    def multiply():
        group = 4
        assert slots % group == 0

        def some(step, carry):
            products = [
                lax.dot_general(
                    work[col_table[step * group + k]],
                    blocks[step * group + k],
                    (((1,), (1,)), ((), ())),
                    preferred_element_type=jnp.float32,
                )
                for k in range(group)
            ]
            for k in range(group):
                sums[step * group + k] = products[k] + sums[prev_table[step * group + k]]
            return carry

        lax.fori_loop(0, slots // group, some, 0, unroll=2)

    def scatter_copies(phase):
        return [
            remote(
                part.at[phase, step - 1], land.at[phase, step - 1],
                p_send.at[phase, step - 1], p_recv.at[phase, step - 1],
                (me_row, col_peer(step)),
            )
            for step in range(1, n_col)
        ]

    def fill_scatter(phase, start):
        copies = scatter_copies(phase) if start else []
        for step in range(1, n_col):
            owner = col_peer(step)
            for p in range(piece):
                part[phase, step - 1, p] = sums[last_table[owner * piece + p]].astype(
                    jnp.bfloat16
                )
            if start:
                copies[step - 1].start()
        for p in range(piece):
            kept[phase, p] = sums[last_table[me_col * piece + p]]

    def finish_scatter(phase, panel, first, target):
        for copy in scatter_copies(phase):
            copy.wait()
        for p in range(piece):
            total = kept[phase, p]
            for step in range(1, n_col):
                total = total + land[phase, step - 1, p].astype(jnp.float32)
            image[target : target + wanted, spot(p)] = (
                panel[first : first + wanted, spot(p)] - scale[:, spot(p)] * total
            )

    def swap_copies(turn, land, send, recv, along_col, source):
        me = me_col if along_col else me_row
        copies = []
        for step in range(1, n_col if along_col else n_row):
            peer = col_peer(step) if along_col else row_peer(step)
            device = (me_row, peer) if along_col else (peer, me_col)
            copies.append(
                remote(
                    source(peer), land.at[turn, me],
                    send.at[turn, step - 1], recv.at[turn, step - 1], device,
                )
            )
        return copies

    def swap(*args):
        copies = swap_copies(*args)
        for copy in copies:
            copy.start()
        for copy in copies:
            copy.wait()

    def total_of(land, turn, count):
        value = land[turn, 0]
        for k in range(1, count):
            value = value + land[turn, k]
        return value

    def add_up(turn, value):
        height = LANES // n_col
        for k in range(n_col):
            own_x[turn, k] = value[k * height : (k + 1) * height]
        cols_x[turn, me_col] = own_x[turn, me_col]
        swap(turn, cols_x, c_send, c_recv, True, lambda peer: own_x.at[turn, peer])
        rows_x[turn, me_row] = total_of(cols_x, turn, n_col)
        swap(turn, rows_x, r_send, r_recv, False, lambda peer: rows_x.at[turn, me_row])
        all_x[turn, me_col] = total_of(rows_x, turn, n_row)
        swap(turn, all_x, a_send, a_recv, True, lambda peer: all_x.at[turn, me_col])
        return jnp.concatenate([all_x[turn, k] for k in range(n_col)], 0)

    pair = slice(0, 2 * wanted)
    third = slice(2 * wanted, 3 * wanted)
    narrow = grid_ids(wanted)[1] < wanted
    half = grid_ids(wanted)[1] < 2 * wanted

    start_gather(0, basis, 0)
    block_copy.wait()
    finish_gather(0)
    start_gather(1, basis, wanted)
    multiply()
    fill_scatter(0, True)
    finish_gather(1)
    multiply()
    fill_scatter(1, False)
    finish_scatter(0, basis, 0, 0)
    moved[0:wanted] = basis[0:wanted] - image[0:wanted]
    moved[wanted:] = jnp.zeros((LANES - wanted, piece * side), jnp.float32)
    start_gather(2, moved, 0)
    for copy in scatter_copies(1):
        copy.start()
    finish_scatter(1, basis, wanted, wanted)

    def pair_swap():
        return swap_copies(
            0, pair_cols, d_send, d_recv, True, lambda peer: pair_cols.at[0, me_col]
        )

    both = jnp.concatenate([basis[pair], image[pair]], 0)
    pair_cols[0, me_col] = dot_nt(basis[pair], both)
    for copy in pair_swap():
        copy.start()

    def find_residual():
        gram_inv = pad_rows(inverse(jnp.where(narrow, gram_ref[0:wanted], 0.0)))
        rayleigh_t = jnp.where(narrow, cross_ref[...].T[0:wanted], 0.0)
        quotient_t = dot(rayleigh_t, gram_inv)
        basis[third] = image[0:wanted] - dot(quotient_t, basis[...])
        return gram_inv, quotient_t

    def iteration(turn, carry):
        finish_gather(turn + 2)
        multiply()
        fill_scatter(turn + 2, True)

        @pl.when(turn == 0)
        def _():
            for copy in pair_swap():
                copy.wait()
            pair_rows[0, me_row] = total_of(pair_cols, 0, n_col)
            swap(0, pair_rows, e_send, e_recv, False, lambda peer: pair_rows.at[0, me_row])
            grams = pad_rows(total_of(pair_rows, 0, n_row))
            gram_ref[...] = jnp.where(col_id < 2 * wanted, grams, 0.0)
            cross_ref[...] = pad_rows(grams.T[2 * wanted :]).T

        gram_inv, quotient_t = find_residual()
        gram_pair = gram_ref[...]
        cross_pair = cross_ref[...]
        pair_inv = extend_inverse(
            gram_inv, jnp.where(half, gram_pair[wanted : 2 * wanted], 0.0), wanted
        )
        turned = basis[third] + dot(quotient_t, moved[...])
        finish_scatter(turn + 2, moved, 0, 2 * wanted)
        image[third] = turned - image[third]
        everything = jnp.concatenate([basis[...], image[...]], 0)
        by_residual = dot_nt(basis[third], everything)
        border = add_up(
            turn,
            pad_rows(
                jnp.concatenate(
                    [
                        by_residual[:, :LANES],
                        by_residual[:, LANES:],
                        dot_nt(image[third], basis[...]),
                    ],
                    0,
                )
            ),
        )

        def around(rows, cols):
            low = pad_rows(rows, 2 * wanted)
            right = pad_rows(cols, 2 * wanted).T
            return low + jnp.where(row_id < 2 * wanted, right, 0.0)

        full_inv = extend_inverse(pair_inv, border[0:wanted], 2 * wanted)
        gram_b = gram_pair + around(border[0:wanted], border[0:wanted])
        cross = cross_pair + around(border[wanted : 2 * wanted], border[third])
        gram_a = 0.5 * (cross + cross.T)
        shifted = cutoff[0] * eye - dot(gram_a, full_inv)
        square = dot(shifted, shifted)
        trace = jnp.sum(
            jnp.sum(jnp.where(row_id == col_id, square, 0.0), axis=1, keepdims=True),
            axis=0,
            keepdims=True,
        )
        norm = 1.0 / jnp.sqrt(trace + 1e-06)
        sign = (1.5 * norm) * shifted - (0.5 * norm) * dot(
            shifted * norm, square * norm
        )

        def newton(_, now):
            return 1.5 * now - 0.5 * dot(now, dot(now, now))

        sign = lax.fori_loop(0, NS_STEPS - 1, newton, sign)
        coeffs = 0.5 * (eye + sign)[0:wanted]
        mixed = jnp.concatenate([coeffs, jnp.where(narrow, 0.0, coeffs)], 0)
        basis[pair] = dot(mixed, basis[...])
        image[pair] = dot(mixed, image[...])

        @pl.when(turn + 1 < ITERS)
        def _():
            moved[0:wanted] = basis[0:wanted] - image[0:wanted]
            start_gather(turn + 3, moved, 0)

        square_mix = pad_rows(mixed)
        gram_ref[...] = dot_nt(dot(square_mix, gram_b), square_mix)
        cross_ref[...] = dot_nt(dot(square_mix, cross), square_mix)
        return carry

    lax.fori_loop(0, ITERS, iteration, 0)
    find_residual()
    out_x[...] = basis[0:wanted]
    out_p[...] = basis[wanted : 2 * wanted]
    out_r[...] = basis[third]
    out_ip[...] = image[wanted : 2 * wanted]


def hand_on(*refs):
    for source, target in zip(refs[:4], refs[4:]):
        target[...] = source[...]


def local(
    n_row, n_col,
    blocks, pattern_rows, pattern_cols, live_count, degree_scale, eigen_block, direction, cutoff,
):
    block_set = blocks[0, 0]
    slots, side, _ = block_set.shape
    wanted, docs = eigen_block.shape
    piece = docs // side
    out_rows = n_col * piece
    row_index = pattern_rows[0, 0]
    slot_id = jnp.arange(slots, dtype=jnp.int32)

    def latest(rows, bound):
        fits = (
            (rows[:, None] == row_index[None, :])
            & (slot_id[None, :] < bound[:, None])
            & (slot_id[None, :] < live_count[0, 0])
        )
        found = jnp.max(jnp.where(fits, slot_id[None, :], -1), axis=1)
        return jnp.where(found < 0, slots, found).astype(jnp.int32)

    previous = latest(row_index, slot_id)
    last = latest(
        jnp.arange(out_rows, dtype=jnp.int32), jnp.full((out_rows,), slots, jnp.int32)
    )

    phases = ITERS + 2
    height = LANES // n_col
    bf16, f32 = jnp.bfloat16, jnp.float32
    sem = pltpu.SemaphoreType.DMA
    vmem = pl.BlockSpec(memory_space=pltpu.VMEM)
    smem = pl.BlockSpec(memory_space=pltpu.SMEM)
    out = jax.ShapeDtypeStruct((wanted, docs), f32)
    results = pl.pallas_call(
        functools.partial(body, n_row, n_col, piece, slots, wanted),
        out_shape=(out, out, out, out),
        in_specs=[smem, smem, smem, smem, pl.BlockSpec(memory_space=pl.ANY), vmem, vmem, vmem],
        out_specs=(vmem, vmem, vmem, vmem),
        scratch_shapes=[
            pltpu.VMEM((slots, side, side), bf16),
            pltpu.VMEM((LANES, docs), f32),
            pltpu.VMEM((LANES, docs), f32),
            pltpu.VMEM((LANES, docs), f32),
            pltpu.VMEM((n_row * piece, wanted, side), bf16),
            pltpu.VMEM((slots + 1, wanted, side), f32),
            pltpu.VMEM((phases, n_row * piece, wanted, side), bf16),
            pltpu.VMEM((phases, n_col - 1, piece, wanted, side), bf16),
            pltpu.VMEM((phases, n_col - 1, piece, wanted, side), bf16),
            pltpu.VMEM((phases, piece, wanted, side), f32),
            pltpu.VMEM((ITERS, n_col, height, LANES), f32),
            pltpu.VMEM((ITERS, n_col, height, LANES), f32),
            pltpu.VMEM((ITERS, n_row, height, LANES), f32),
            pltpu.VMEM((ITERS, n_col, height, LANES), f32),
            pltpu.VMEM((1, n_col, 2 * wanted, LANES), f32),
            pltpu.VMEM((1, n_row, 2 * wanted, LANES), f32),
            pltpu.VMEM((LANES, LANES), f32),
            pltpu.VMEM((LANES, LANES), f32),
            sem,
            sem((phases, n_row - 1)),
            sem((phases, n_row - 1)),
            sem((phases, n_col - 1)),
            sem((phases, n_col - 1)),
            sem((ITERS, n_col - 1)),
            sem((ITERS, n_col - 1)),
            sem((ITERS, n_row - 1)),
            sem((ITERS, n_row - 1)),
            sem((ITERS, n_col - 1)),
            sem((ITERS, n_col - 1)),
            sem((1, n_col - 1)),
            sem((1, n_col - 1)),
            sem((1, n_row - 1)),
            sem((1, n_row - 1)),
        ],
        compiler_params=pltpu.CompilerParams(
            collective_id=0, has_side_effects=True, vmem_limit_bytes=56 * 1024 * 1024
        ),
    )(pattern_cols[0, 0], previous, last, cutoff, block_set, degree_scale, eigen_block, direction)
    return pl.pallas_call(
        hand_on,
        out_shape=(out, out, out, out),
        in_specs=[vmem] * 4,
        out_specs=(vmem, vmem, vmem, vmem),
    )(*results)


def solution(mesh):
    placed = (
        P("brow", "bcol", None, None, None),
        P("brow", "bcol", None),
        P("brow", "bcol", None),
        P("brow", "bcol"),
        P(("brow", "bcol")),
        P(None, ("brow", "bcol")),
        P(None, ("brow", "bcol")),
        P(),
    )
    return jax.shard_map(
        functools.partial(local, mesh.shape["brow"], mesh.shape["bcol"]),
        mesh=mesh,
        in_specs=placed,
        out_specs=(
            P(None, ("brow", "bcol")),
            P(None, ("brow", "bcol")),
            P(None, ("brow", "bcol")),
            P(None, ("brow", "bcol")),
        ),
        check_vma=False,
    )
```

```python
import functools

import jax
import jax.numpy as jnp
from jax import lax
from jax.experimental import pallas as pl
from jax.experimental.pallas import tpu as pltpu
from jax.sharding import PartitionSpec as P

ITERS = 2
NS_STEPS = 8
MESH = pl.DeviceIdType.MESH
LANES = 128


def halves(value):
    high = value.astype(jnp.bfloat16)
    return high, (value - high.astype(jnp.float32)).astype(jnp.bfloat16)


def split_dot(left, right, right_dim):
    rows = left.shape[0]
    left_high, left_low = halves(left)
    right_high, right_low = halves(right)

    def part(first, second):
        return lax.dot_general(
            first,
            second,
            (((1,), (right_dim,)), ((), ())),
            preferred_element_type=jnp.float32,
        )

    main = part(jnp.concatenate([left_high, left_low], 0), right_high)
    return main[:rows] + (main[rows:] + part(left_high, right_low))


def dot(left, right):
    return split_dot(left, right, 0)


def dot_nt(left, right):
    return split_dot(left, right, 1)


def grid_ids(rows):
    shape = (rows, LANES)
    return (
        lax.broadcasted_iota(jnp.int32, shape, 0),
        lax.broadcasted_iota(jnp.int32, shape, 1),
    )


def pad_rows(value, before=0):
    parts = [value, jnp.zeros((LANES - before - value.shape[0], LANES), jnp.float32)]
    if before:
        parts.insert(0, jnp.zeros((before, LANES), jnp.float32))
    return jnp.concatenate(parts, 0)


def inverse_pair(a, b, d):
    scale = 1.0 / (a * d - b * b)
    return d * scale, -(b * scale), a * scale


def inverse_four(m):
    p, q, r = inverse_pair(m[0][0], m[0][1], m[1][1])
    e = [[p * m[0][2 + c] + q * m[1][2 + c] for c in range(2)],
         [q * m[0][2 + c] + r * m[1][2 + c] for c in range(2)]]

    def schur(i, j):
        return m[2 + i][2 + j] - (m[0][2 + i] * e[0][j] + m[1][2 + i] * e[1][j])

    x, y, z = inverse_pair(schur(0, 0), schur(0, 1), schur(1, 1))
    f = [[e[i][0] * x + e[i][1] * y, e[i][0] * y + e[i][1] * z] for i in range(2)]

    def corner(i, j):
        return f[i][0] * e[j][0] + f[i][1] * e[j][1]

    off = q + corner(0, 1)
    return [
        [p + corner(0, 0), off, -f[0][0], -f[0][1]],
        [off, r + corner(1, 1), -f[1][0], -f[1][1]],
        [-f[0][0], -f[1][0], x, y],
        [-f[0][1], -f[1][1], y, z],
    ]


def inverse(matrix):
    side = matrix.shape[0]
    row_id, col_id = grid_ids(side)
    width = 4
    assert side % width == 0

    def sweep(step, now):
        first = step * width
        at_row = [row_id == first + k for k in range(width)]
        at_col = [col_id == first + k for k in range(width)]
        cols = [
            jnp.sum(jnp.where(at_col[k], now, 0.0), axis=1, keepdims=True)
            for k in range(width)
        ]
        rows = [
            jnp.sum(jnp.where(at_row[k], now, 0.0), axis=0, keepdims=True)
            for k in range(width)
        ]
        wide = [jnp.broadcast_to(col, now.shape) for col in cols]
        pivots = [
            [
                jnp.sum(jnp.where(at_row[i], wide[j], 0.0), axis=0, keepdims=True)
                for j in range(width)
            ]
            for i in range(width)
        ]
        inner = inverse_four(pivots)
        scaled_rows = [
            (inner[i][0] * rows[0] + inner[i][1] * rows[1])
            + (inner[i][2] * rows[2] + inner[i][3] * rows[3])
            for i in range(width)
        ]
        out = now - (
            (wide[0] * scaled_rows[0] + wide[1] * scaled_rows[1])
            + (wide[2] * scaled_rows[2] + wide[3] * scaled_rows[3])
        )
        for i in range(width):
            scaled_col = (wide[0] * inner[0][i] + wide[1] * inner[1][i]) + (
                wide[2] * inner[2][i] + wide[3] * inner[3][i]
            )
            out = jnp.where(at_col[i], scaled_col, out)
        for i in range(width):
            line = scaled_rows[i]
            for j in range(width):
                line = jnp.where(at_col[j][0:1], -inner[i][j], line)
            out = jnp.where(at_row[i], line, out)
        return out

    return -lax.fori_loop(0, side // width, sweep, matrix)


def extend_inverse(known, border, offset):
    side = border.shape[0]
    row_id, col_id = grid_ids(side)
    placed = (col_id == row_id + offset).astype(jnp.float32)
    edge = pad_rows(placed - dot(border, known))
    middle = inverse(dot_nt(border, edge))
    return known + dot(edge.T, pad_rows(dot(middle, edge)))


def body(
    n_row, n_col, piece, slots, wanted,
    row_table, col_table, live_ref, cutoff, blocks_hbm, scale_ref, eigen_ref, direction_ref,
    out_x, out_p, out_r, out_ip,
    prev_table, last_table, blocks, basis, image, moved, work, sums, gather, part, land, kept,
    own_x, cols_x, rows_x, all_x, pair_cols, pair_rows, gram_ref, cross_ref,
    block_sem, g_send, g_recv, p_send, p_recv,
    c_send, c_recv, r_send, r_recv, a_send, a_recv, d_send, d_recv, e_send, e_recv,
):
    me_row, me_col = lax.axis_index("brow"), lax.axis_index("bcol")
    side = blocks.shape[-1]
    block_copy = pltpu.make_async_copy(blocks_hbm, blocks, block_sem)
    block_copy.start()

    def row_peer(step):
        return lax.rem(me_row + step, n_row)

    def col_peer(step):
        return lax.rem(me_col + step, n_col)

    barrier = pltpu.get_barrier_semaphore()
    for step in range(1, n_row):
        pl.semaphore_signal(
            barrier, inc=1, device_id=(row_peer(step), me_col), device_id_type=MESH
        )
    for step in range(1, n_col):
        pl.semaphore_signal(
            barrier, inc=1, device_id=(me_row, col_peer(step)), device_id_type=MESH
        )

    scale = scale_ref[...].reshape(1, piece * side)
    basis[0:wanted] = eigen_ref[...]
    basis[wanted : 2 * wanted] = direction_ref[...]
    basis[2 * wanted :] = jnp.zeros((LANES - 2 * wanted, piece * side), jnp.float32)
    image[...] = jnp.zeros(image.shape, jnp.float32)
    sums[slots] = jnp.zeros(sums.shape[1:], jnp.float32)

    pl.semaphore_wait(barrier, n_row + n_col - 2)
    row_id, col_id = grid_ids(LANES)
    eye = jnp.where((row_id == col_id) & (row_id < 3 * wanted), 1.0, 0.0)

    def remote(src, dst, send, recv, device):
        return pltpu.make_async_remote_copy(
            src_ref=src, dst_ref=dst, send_sem=send, recv_sem=recv,
            device_id=device, device_id_type=MESH,
        )

    def spot(p):
        return slice(p * side, (p + 1) * side)

    def gather_copies(phase):
        mine = pl.ds(me_row * piece, piece)
        return [
            remote(
                gather.at[phase, mine], gather.at[phase, mine],
                g_send.at[phase, step - 1], g_recv.at[phase, step - 1],
                (row_peer(step), me_col),
            )
            for step in range(1, n_row)
        ]

    def start_gather(phase, panel, first):
        for p in range(piece):
            gather[phase, me_row * piece + p] = (
                scale[:, spot(p)] * panel[first : first + wanted, spot(p)]
            ).astype(jnp.bfloat16)
        for copy in gather_copies(phase):
            copy.start()

    def finish_gather(phase):
        for copy in gather_copies(phase):
            copy.wait()

        def move(k, carry):
            work[k] = gather[phase, k]
            return carry

        lax.fori_loop(0, n_row * piece, move, 0, unroll=4)

    def latest(row, bound):
        limit = jnp.minimum(bound, live_ref[0, 0])
        found = jnp.int32(slots)
        for k in range(slots):
            found = jnp.where((row_table[k] == row) & (k < limit), jnp.int32(k), found)
        return found

    def fill_previous(s, carry):
        prev_table[s] = latest(row_table[s], s)
        return carry

    def fill_last(row, carry):
        last_table[row] = latest(row, slots)
        return carry

    def turn_block(s, carry):
        blocks[s] = blocks[s].T
        return carry

    def multiply():
        group = 4
        assert slots % group == 0

        def some(step, carry):
            products = [
                lax.dot_general(
                    work[col_table[step * group + k]],
                    blocks[step * group + k],
                    (((1,), (0,)), ((), ())),
                    preferred_element_type=jnp.float32,
                )
                for k in range(group)
            ]
            for k in range(group):
                sums[step * group + k] = products[k] + sums[prev_table[step * group + k]]
            return carry

        lax.fori_loop(0, slots // group, some, 0, unroll=2)

    def scatter_copies(phase):
        return [
            remote(
                part.at[phase, step - 1], land.at[phase, step - 1],
                p_send.at[phase, step - 1], p_recv.at[phase, step - 1],
                (me_row, col_peer(step)),
            )
            for step in range(1, n_col)
        ]

    def fill_scatter(phase, start):
        copies = scatter_copies(phase) if start else []
        for step in range(1, n_col):
            owner = col_peer(step)
            for p in range(piece):
                part[phase, step - 1, p] = sums[last_table[owner * piece + p]].astype(
                    jnp.bfloat16
                )
            if start:
                copies[step - 1].start()
        for p in range(piece):
            kept[phase, p] = sums[last_table[me_col * piece + p]]

    def finish_scatter(phase, panel, first, target):
        for copy in scatter_copies(phase):
            copy.wait()
        for p in range(piece):
            total = kept[phase, p]
            for step in range(1, n_col):
                total = total + land[phase, step - 1, p].astype(jnp.float32)
            image[target : target + wanted, spot(p)] = (
                panel[first : first + wanted, spot(p)] - scale[:, spot(p)] * total
            )

    def swap_copies(turn, land, send, recv, along_col, source):
        me = me_col if along_col else me_row
        copies = []
        for step in range(1, n_col if along_col else n_row):
            peer = col_peer(step) if along_col else row_peer(step)
            device = (me_row, peer) if along_col else (peer, me_col)
            copies.append(
                remote(
                    source(peer), land.at[turn, me],
                    send.at[turn, step - 1], recv.at[turn, step - 1], device,
                )
            )
        return copies

    def swap(*args):
        copies = swap_copies(*args)
        for copy in copies:
            copy.start()
        for copy in copies:
            copy.wait()

    def total_of(land, turn, count):
        value = land[turn, 0]
        for k in range(1, count):
            value = value + land[turn, k]
        return value

    def add_up(turn, value):
        height = LANES // n_col
        for k in range(n_col):
            own_x[turn, k] = value[k * height : (k + 1) * height]
        cols_x[turn, me_col] = own_x[turn, me_col]
        swap(turn, cols_x, c_send, c_recv, True, lambda peer: own_x.at[turn, peer])
        rows_x[turn, me_row] = total_of(cols_x, turn, n_col)
        swap(turn, rows_x, r_send, r_recv, False, lambda peer: rows_x.at[turn, me_row])
        all_x[turn, me_col] = total_of(rows_x, turn, n_row)
        swap(turn, all_x, a_send, a_recv, True, lambda peer: all_x.at[turn, me_col])
        return jnp.concatenate([all_x[turn, k] for k in range(n_col)], 0)

    pair = slice(0, 2 * wanted)
    third = slice(2 * wanted, 3 * wanted)
    narrow = grid_ids(wanted)[1] < wanted
    half = grid_ids(wanted)[1] < 2 * wanted

    start_gather(0, basis, 0)
    lax.fori_loop(0, slots, fill_previous, 0)
    lax.fori_loop(0, n_col * piece, fill_last, 0)
    block_copy.wait()
    lax.fori_loop(0, slots, turn_block, 0, unroll=2)
    finish_gather(0)
    start_gather(1, basis, wanted)
    multiply()
    fill_scatter(0, True)
    finish_gather(1)
    multiply()
    fill_scatter(1, False)
    finish_scatter(0, basis, 0, 0)
    moved[0:wanted] = basis[0:wanted] - image[0:wanted]
    moved[wanted:] = jnp.zeros((LANES - wanted, piece * side), jnp.float32)
    start_gather(2, moved, 0)
    for copy in scatter_copies(1):
        copy.start()
    finish_scatter(1, basis, wanted, wanted)

    def pair_swap():
        return swap_copies(
            0, pair_cols, d_send, d_recv, True, lambda peer: pair_cols.at[0, me_col]
        )

    both = jnp.concatenate([basis[pair], image[pair]], 0)
    pair_cols[0, me_col] = dot_nt(basis[pair], both)
    for copy in pair_swap():
        copy.start()

    def find_residual():
        gram_inv = pad_rows(inverse(jnp.where(narrow, gram_ref[0:wanted], 0.0)))
        rayleigh_t = jnp.where(narrow, cross_ref[...].T[0:wanted], 0.0)
        quotient_t = dot(rayleigh_t, gram_inv)
        basis[third] = image[0:wanted] - dot(quotient_t, basis[...])
        return gram_inv, quotient_t

    def iteration(turn, carry):
        finish_gather(turn + 2)
        multiply()
        fill_scatter(turn + 2, True)

        @pl.when(turn == 0)
        def _():
            for copy in pair_swap():
                copy.wait()
            pair_rows[0, me_row] = total_of(pair_cols, 0, n_col)
            swap(0, pair_rows, e_send, e_recv, False, lambda peer: pair_rows.at[0, me_row])
            grams = pad_rows(total_of(pair_rows, 0, n_row))
            gram_ref[...] = jnp.where(col_id < 2 * wanted, grams, 0.0)
            cross_ref[...] = pad_rows(grams.T[2 * wanted :]).T

        gram_inv, quotient_t = find_residual()
        gram_pair = gram_ref[...]
        cross_pair = cross_ref[...]
        pair_inv = extend_inverse(
            gram_inv, jnp.where(half, gram_pair[wanted : 2 * wanted], 0.0), wanted
        )
        turned = basis[third] + dot(quotient_t, moved[...])
        finish_scatter(turn + 2, moved, 0, 2 * wanted)
        image[third] = turned - image[third]
        everything = jnp.concatenate([basis[...], image[...]], 0)
        by_residual = dot_nt(basis[third], everything)
        border = add_up(
            turn,
            pad_rows(
                jnp.concatenate(
                    [
                        by_residual[:, :LANES],
                        by_residual[:, LANES:],
                        dot_nt(image[third], basis[...]),
                    ],
                    0,
                )
            ),
        )

        def around(rows, cols):
            low = pad_rows(rows, 2 * wanted)
            right = pad_rows(cols, 2 * wanted).T
            return low + jnp.where(row_id < 2 * wanted, right, 0.0)

        full_inv = extend_inverse(pair_inv, border[0:wanted], 2 * wanted)
        gram_b = gram_pair + around(border[0:wanted], border[0:wanted])
        cross = cross_pair + around(border[wanted : 2 * wanted], border[third])
        gram_a = 0.5 * (cross + cross.T)
        shifted = cutoff[0] * eye - dot(gram_a, full_inv)
        square = dot(shifted, shifted)
        trace = jnp.sum(
            jnp.sum(jnp.where(row_id == col_id, square, 0.0), axis=1, keepdims=True),
            axis=0,
            keepdims=True,
        )
        norm = 1.0 / jnp.sqrt(trace + 1e-06)
        sign = (1.5 * norm) * shifted - (0.5 * norm) * dot(
            shifted * norm, square * norm
        )

        def newton(_, now):
            return 1.5 * now - 0.5 * dot(now, dot(now, now))

        sign = lax.fori_loop(0, NS_STEPS - 1, newton, sign)
        coeffs = 0.5 * (eye + sign)[0:wanted]
        mixed = jnp.concatenate([coeffs, jnp.where(narrow, 0.0, coeffs)], 0)
        basis[pair] = dot(mixed, basis[...])
        image[pair] = dot(mixed, image[...])

        @pl.when(turn + 1 < ITERS)
        def _():
            moved[0:wanted] = basis[0:wanted] - image[0:wanted]
            start_gather(turn + 3, moved, 0)

        square_mix = pad_rows(mixed)
        gram_ref[...] = dot_nt(dot(square_mix, gram_b), square_mix)
        cross_ref[...] = dot_nt(dot(square_mix, cross), square_mix)
        return carry

    lax.fori_loop(0, ITERS, iteration, 0)
    find_residual()
    out_x[...] = basis[0:wanted]
    out_p[...] = basis[wanted : 2 * wanted]
    out_r[...] = basis[third]
    out_ip[...] = image[wanted : 2 * wanted]


def hand_on(*refs):
    for source, target in zip(refs[:4], refs[4:]):
        target[...] = source[...]


def local(
    n_row, n_col,
    blocks, pattern_rows, pattern_cols, live_count, degree_scale, eigen_block, direction, cutoff,
):
    block_set = blocks[0, 0]
    slots, side, _ = block_set.shape
    wanted, docs = eigen_block.shape
    piece = docs // side
    out_rows = n_col * piece
    phases = ITERS + 2
    height = LANES // n_col
    bf16, f32 = jnp.bfloat16, jnp.float32
    sem = pltpu.SemaphoreType.DMA
    vmem = pl.BlockSpec(memory_space=pltpu.VMEM)
    smem = pl.BlockSpec(memory_space=pltpu.SMEM)
    out = jax.ShapeDtypeStruct((wanted, docs), f32)
    results = pl.pallas_call(
        functools.partial(body, n_row, n_col, piece, slots, wanted),
        out_shape=(out, out, out, out),
        in_specs=[smem, smem, smem, smem, pl.BlockSpec(memory_space=pl.ANY), vmem, vmem, vmem],
        out_specs=(vmem, vmem, vmem, vmem),
        scratch_shapes=[
            pltpu.SMEM((slots,), jnp.int32),
            pltpu.SMEM((out_rows,), jnp.int32),
            pltpu.VMEM((slots, side, side), bf16),
            pltpu.VMEM((LANES, docs), f32),
            pltpu.VMEM((LANES, docs), f32),
            pltpu.VMEM((LANES, docs), f32),
            pltpu.VMEM((n_row * piece, wanted, side), bf16),
            pltpu.VMEM((slots + 1, wanted, side), f32),
            pltpu.VMEM((phases, n_row * piece, wanted, side), bf16),
            pltpu.VMEM((phases, n_col - 1, piece, wanted, side), bf16),
            pltpu.VMEM((phases, n_col - 1, piece, wanted, side), bf16),
            pltpu.VMEM((phases, piece, wanted, side), f32),
            pltpu.VMEM((ITERS, n_col, height, LANES), f32),
            pltpu.VMEM((ITERS, n_col, height, LANES), f32),
            pltpu.VMEM((ITERS, n_row, height, LANES), f32),
            pltpu.VMEM((ITERS, n_col, height, LANES), f32),
            pltpu.VMEM((1, n_col, 2 * wanted, LANES), f32),
            pltpu.VMEM((1, n_row, 2 * wanted, LANES), f32),
            pltpu.VMEM((LANES, LANES), f32),
            pltpu.VMEM((LANES, LANES), f32),
            sem,
            sem((phases, n_row - 1)),
            sem((phases, n_row - 1)),
            sem((phases, n_col - 1)),
            sem((phases, n_col - 1)),
            sem((ITERS, n_col - 1)),
            sem((ITERS, n_col - 1)),
            sem((ITERS, n_row - 1)),
            sem((ITERS, n_row - 1)),
            sem((ITERS, n_col - 1)),
            sem((ITERS, n_col - 1)),
            sem((1, n_col - 1)),
            sem((1, n_col - 1)),
            sem((1, n_row - 1)),
            sem((1, n_row - 1)),
        ],
        compiler_params=pltpu.CompilerParams(
            collective_id=0, has_side_effects=True, vmem_limit_bytes=56 * 1024 * 1024
        ),
    )(pattern_rows[0, 0], pattern_cols[0, 0], live_count, cutoff, block_set, degree_scale, eigen_block, direction)
    return pl.pallas_call(
        hand_on,
        out_shape=(out, out, out, out),
        in_specs=[vmem] * 4,
        out_specs=(vmem, vmem, vmem, vmem),
    )(*results)


def solution(mesh):
    placed = (
        P("brow", "bcol", None, None, None),
        P("brow", "bcol", None),
        P("brow", "bcol", None),
        P("brow", "bcol"),
        P(("brow", "bcol")),
        P(None, ("brow", "bcol")),
        P(None, ("brow", "bcol")),
        P(),
    )
    return jax.shard_map(
        functools.partial(local, mesh.shape["brow"], mesh.shape["bcol"]),
        mesh=mesh,
        in_specs=placed,
        out_specs=(
            P(None, ("brow", "bcol")),
            P(None, ("brow", "bcol")),
            P(None, ("brow", "bcol")),
            P(None, ("brow", "bcol")),
        ),
        check_vma=False,
    )
```

```python
import functools

import jax
import jax.numpy as jnp
from jax import lax
from jax.experimental import pallas as pl
from jax.experimental.pallas import tpu as pltpu
from jax.sharding import PartitionSpec as P

ITERS = 2
NS_STEPS = 8
MESH = pl.DeviceIdType.MESH
LANES = 128


def halves(value):
    high = value.astype(jnp.bfloat16)
    return high, (value - high.astype(jnp.float32)).astype(jnp.bfloat16)


def split_dot(left, right, right_dim):
    rows = left.shape[0]
    left_high, left_low = halves(left)
    right_high, right_low = halves(right)

    def part(first, second):
        return lax.dot_general(
            first,
            second,
            (((1,), (right_dim,)), ((), ())),
            preferred_element_type=jnp.float32,
        )

    main = part(jnp.concatenate([left_high, left_low], 0), right_high)
    return main[:rows] + (main[rows:] + part(left_high, right_low))


def dot(left, right):
    return split_dot(left, right, 0)


def dot_nt(left, right):
    return split_dot(left, right, 1)


def grid_ids(rows):
    shape = (rows, LANES)
    return (
        lax.broadcasted_iota(jnp.int32, shape, 0),
        lax.broadcasted_iota(jnp.int32, shape, 1),
    )


def pad_rows(value, before=0):
    parts = [value, jnp.zeros((LANES - before - value.shape[0], LANES), jnp.float32)]
    if before:
        parts.insert(0, jnp.zeros((before, LANES), jnp.float32))
    return jnp.concatenate(parts, 0)


def inverse_pair(a, b, d):
    scale = 1.0 / (a * d - b * b)
    return d * scale, -(b * scale), a * scale


def inverse_four(m):
    p, q, r = inverse_pair(m[0][0], m[0][1], m[1][1])
    e = [[p * m[0][2 + c] + q * m[1][2 + c] for c in range(2)],
         [q * m[0][2 + c] + r * m[1][2 + c] for c in range(2)]]

    def schur(i, j):
        return m[2 + i][2 + j] - (m[0][2 + i] * e[0][j] + m[1][2 + i] * e[1][j])

    x, y, z = inverse_pair(schur(0, 0), schur(0, 1), schur(1, 1))
    f = [[e[i][0] * x + e[i][1] * y, e[i][0] * y + e[i][1] * z] for i in range(2)]

    def corner(i, j):
        return f[i][0] * e[j][0] + f[i][1] * e[j][1]

    off = q + corner(0, 1)
    return [
        [p + corner(0, 0), off, -f[0][0], -f[0][1]],
        [off, r + corner(1, 1), -f[1][0], -f[1][1]],
        [-f[0][0], -f[1][0], x, y],
        [-f[0][1], -f[1][1], y, z],
    ]


def inverse(matrix):
    side = matrix.shape[0]
    row_id, col_id = grid_ids(side)
    width = 4
    assert side % width == 0

    def sweep(step, now):
        first = step * width
        at_row = [row_id == first + k for k in range(width)]
        at_col = [col_id == first + k for k in range(width)]
        cols = [
            jnp.sum(jnp.where(at_col[k], now, 0.0), axis=1, keepdims=True)
            for k in range(width)
        ]
        rows = [
            jnp.sum(jnp.where(at_row[k], now, 0.0), axis=0, keepdims=True)
            for k in range(width)
        ]
        wide = [jnp.broadcast_to(col, now.shape) for col in cols]
        pivots = [
            [
                jnp.sum(jnp.where(at_row[i], wide[j], 0.0), axis=0, keepdims=True)
                for j in range(width)
            ]
            for i in range(width)
        ]
        inner = inverse_four(pivots)
        scaled_rows = [
            (inner[i][0] * rows[0] + inner[i][1] * rows[1])
            + (inner[i][2] * rows[2] + inner[i][3] * rows[3])
            for i in range(width)
        ]
        out = now - (
            (wide[0] * scaled_rows[0] + wide[1] * scaled_rows[1])
            + (wide[2] * scaled_rows[2] + wide[3] * scaled_rows[3])
        )
        for i in range(width):
            scaled_col = (wide[0] * inner[0][i] + wide[1] * inner[1][i]) + (
                wide[2] * inner[2][i] + wide[3] * inner[3][i]
            )
            out = jnp.where(at_col[i], scaled_col, out)
        for i in range(width):
            line = scaled_rows[i]
            for j in range(width):
                line = jnp.where(at_col[j][0:1], -inner[i][j], line)
            out = jnp.where(at_row[i], line, out)
        return out

    return -lax.fori_loop(0, side // width, sweep, matrix)


def extend_inverse(known, border, offset):
    side = border.shape[0]
    row_id, col_id = grid_ids(side)
    placed = (col_id == row_id + offset).astype(jnp.float32)
    edge = pad_rows(placed - dot(border, known))
    middle = inverse(dot_nt(border, edge))
    return known + dot(edge.T, pad_rows(dot(middle, edge)))


def body(
    n_row, n_col, piece, slots, wanted,
    row_table, col_table, live_ref, cutoff, blocks_hbm, scale_ref, eigen_ref, direction_ref,
    out_x, out_p, out_r, out_ip,
    prev_table, last_table, blocks, basis, image, moved, work, sums, gather, part, land, kept,
    own_x, cols_x, rows_x, all_x, pair_cols, pair_rows, gram_ref, cross_ref,
    block_sem, g_send, g_recv, p_send, p_recv,
    c_send, c_recv, r_send, r_recv, a_send, a_recv, d_send, d_recv, e_send, e_recv,
):
    me_row, me_col = lax.axis_index("brow"), lax.axis_index("bcol")
    side = blocks.shape[-1]
    block_copy = pltpu.make_async_copy(blocks_hbm, blocks, block_sem)
    block_copy.start()

    def row_peer(step):
        return lax.rem(me_row + step, n_row)

    def col_peer(step):
        return lax.rem(me_col + step, n_col)

    barrier = pltpu.get_barrier_semaphore()
    for step in range(1, n_row):
        pl.semaphore_signal(
            barrier, inc=1, device_id=(row_peer(step), me_col), device_id_type=MESH
        )
    for step in range(1, n_col):
        pl.semaphore_signal(
            barrier, inc=1, device_id=(me_row, col_peer(step)), device_id_type=MESH
        )

    scale = scale_ref[...].reshape(1, piece * side)
    basis[0:wanted] = eigen_ref[...]
    basis[wanted : 2 * wanted] = direction_ref[...]
    basis[2 * wanted :] = jnp.zeros((LANES - 2 * wanted, piece * side), jnp.float32)
    image[...] = jnp.zeros(image.shape, jnp.float32)
    sums[slots] = jnp.zeros(sums.shape[1:], jnp.float32)

    pl.semaphore_wait(barrier, n_row + n_col - 2)
    row_id, col_id = grid_ids(LANES)
    eye = jnp.where((row_id == col_id) & (row_id < 3 * wanted), 1.0, 0.0)

    def remote(src, dst, send, recv, device):
        return pltpu.make_async_remote_copy(
            src_ref=src, dst_ref=dst, send_sem=send, recv_sem=recv,
            device_id=device, device_id_type=MESH,
        )

    def spot(p):
        return slice(p * side, (p + 1) * side)

    def gather_copies(phase):
        mine = pl.ds(me_row * piece, piece)
        return [
            remote(
                gather.at[phase, mine], gather.at[phase, mine],
                g_send.at[phase, step - 1], g_recv.at[phase, step - 1],
                (row_peer(step), me_col),
            )
            for step in range(1, n_row)
        ]

    def start_gather(phase, panel, first):
        for p in range(piece):
            gather[phase, me_row * piece + p] = (
                scale[:, spot(p)] * panel[first : first + wanted, spot(p)]
            ).astype(jnp.bfloat16)
        for copy in gather_copies(phase):
            copy.start()

    def finish_gather(phase):
        for copy in gather_copies(phase):
            copy.wait()

        def move(k, carry):
            work[k] = gather[phase, k]
            return carry

        lax.fori_loop(0, n_row * piece, move, 0, unroll=4)

    def latest(row, bound):
        limit = jnp.minimum(bound, live_ref[0, 0])
        found = jnp.int32(slots)
        for k in range(slots):
            found = jnp.where((row_table[k] == row) & (k < limit), jnp.int32(k), found)
        return found

    def fill_previous(s, carry):
        prev_table[s] = latest(row_table[s], s)
        return carry

    def fill_last(row, carry):
        last_table[row] = latest(row, slots)
        return carry

    def turn_block(s, carry):
        blocks[s] = blocks[s].T
        return carry

    def multiply():
        group = 4
        assert slots % group == 0

        def some(step, carry):
            products = [
                lax.dot_general(
                    work[col_table[step * group + k]],
                    blocks[step * group + k],
                    (((1,), (0,)), ((), ())),
                    preferred_element_type=jnp.float32,
                )
                for k in range(group)
            ]
            for k in range(group):
                sums[step * group + k] = products[k] + sums[prev_table[step * group + k]]
            return carry

        lax.fori_loop(0, slots // group, some, 0, unroll=2)

    def scatter_copies(phase):
        return [
            remote(
                part.at[phase, step - 1], land.at[phase, step - 1],
                p_send.at[phase, step - 1], p_recv.at[phase, step - 1],
                (me_row, col_peer(step)),
            )
            for step in range(1, n_col)
        ]

    def fill_scatter(phase, start):
        copies = scatter_copies(phase) if start else []
        for step in range(1, n_col):
            owner = col_peer(step)
            for p in range(piece):
                part[phase, step - 1, p] = sums[last_table[owner * piece + p]].astype(
                    jnp.bfloat16
                )
            if start:
                copies[step - 1].start()
        for p in range(piece):
            kept[phase, p] = sums[last_table[me_col * piece + p]]

    def finish_scatter(phase, panel, first, target):
        for copy in scatter_copies(phase):
            copy.wait()
        for p in range(piece):
            total = kept[phase, p]
            for step in range(1, n_col):
                total = total + land[phase, step - 1, p].astype(jnp.float32)
            image[target : target + wanted, spot(p)] = (
                panel[first : first + wanted, spot(p)] - scale[:, spot(p)] * total
            )

    def swap_copies(turn, land, send, recv, along_col, source):
        me = me_col if along_col else me_row
        copies = []
        for step in range(1, n_col if along_col else n_row):
            peer = col_peer(step) if along_col else row_peer(step)
            device = (me_row, peer) if along_col else (peer, me_col)
            copies.append(
                remote(
                    source(peer), land.at[turn, me],
                    send.at[turn, step - 1], recv.at[turn, step - 1], device,
                )
            )
        return copies

    def swap(*args):
        copies = swap_copies(*args)
        for copy in copies:
            copy.start()
        for copy in copies:
            copy.wait()

    def total_of(land, turn, count):
        value = land[turn, 0]
        for k in range(1, count):
            value = value + land[turn, k]
        return value

    def add_up(turn, value):
        height = LANES // n_col
        for k in range(n_col):
            own_x[turn, k] = value[k * height : (k + 1) * height]
        cols_x[turn, me_col] = own_x[turn, me_col]
        swap(turn, cols_x, c_send, c_recv, True, lambda peer: own_x.at[turn, peer])
        rows_x[turn, me_row] = total_of(cols_x, turn, n_col)
        swap(turn, rows_x, r_send, r_recv, False, lambda peer: rows_x.at[turn, me_row])
        all_x[turn, me_col] = total_of(rows_x, turn, n_row)
        swap(turn, all_x, a_send, a_recv, True, lambda peer: all_x.at[turn, me_col])
        return jnp.concatenate([all_x[turn, k] for k in range(n_col)], 0)

    pair = slice(0, 2 * wanted)
    third = slice(2 * wanted, 3 * wanted)
    narrow = grid_ids(wanted)[1] < wanted
    half = grid_ids(wanted)[1] < 2 * wanted

    start_gather(0, basis, 0)
    lax.fori_loop(0, slots, fill_previous, 0)
    lax.fori_loop(0, n_col * piece, fill_last, 0)
    block_copy.wait()
    lax.fori_loop(0, slots, turn_block, 0, unroll=2)
    finish_gather(0)
    start_gather(1, basis, wanted)
    multiply()
    fill_scatter(0, True)
    finish_gather(1)
    multiply()
    fill_scatter(1, False)
    finish_scatter(0, basis, 0, 0)
    moved[0:wanted] = basis[0:wanted] - image[0:wanted]
    start_gather(2, moved, 0)
    for copy in scatter_copies(1):
        copy.start()
    finish_scatter(1, basis, wanted, wanted)

    def pair_swap():
        return swap_copies(
            0, pair_cols, d_send, d_recv, True, lambda peer: pair_cols.at[0, me_col]
        )

    both = jnp.concatenate([basis[pair], image[pair]], 0)
    pair_cols[0, me_col] = dot_nt(basis[pair], both)
    for copy in pair_swap():
        copy.start()

    def find_residual():
        gram_inv = pad_rows(inverse(jnp.where(narrow, gram_ref[0:wanted], 0.0)))
        rayleigh_t = jnp.where(narrow, cross_ref[...].T[0:wanted], 0.0)
        quotient_t = dot(rayleigh_t, gram_inv)
        quotient_t = quotient_t[:, :wanted]
        basis[third] = image[0:wanted] - dot(quotient_t, basis[0:wanted])
        return gram_inv, quotient_t

    def iteration(turn, carry):
        finish_gather(turn + 2)
        multiply()
        fill_scatter(turn + 2, True)

        @pl.when(turn == 0)
        def _():
            for copy in pair_swap():
                copy.wait()
            pair_rows[0, me_row] = total_of(pair_cols, 0, n_col)
            swap(0, pair_rows, e_send, e_recv, False, lambda peer: pair_rows.at[0, me_row])
            grams = pad_rows(total_of(pair_rows, 0, n_row))
            gram_ref[...] = jnp.where(col_id < 2 * wanted, grams, 0.0)
            cross_ref[...] = pad_rows(grams.T[2 * wanted :]).T

        gram_inv, quotient_t = find_residual()
        gram_pair = gram_ref[...]
        cross_pair = cross_ref[...]
        pair_inv = extend_inverse(
            gram_inv, jnp.where(half, gram_pair[wanted : 2 * wanted], 0.0), wanted
        )
        turned = basis[third] + dot(quotient_t, moved[...])
        by_residual = dot_nt(basis[third], jnp.concatenate([basis[...], image[...]], 0))
        finish_scatter(turn + 2, moved, 0, 2 * wanted)
        image[third] = turned - image[third]
        border = add_up(
            turn,
            pad_rows(
                jnp.concatenate(
                    [
                        by_residual[:, :LANES],
                        jnp.where(half, by_residual[:, LANES:], 0.0),
                        dot_nt(image[third], basis[...]),
                    ],
                    0,
                )
            ),
        )

        full_inv = extend_inverse(pair_inv, border[0:wanted], 2 * wanted)
        low = pad_rows(border[0:wanted], 2 * wanted)
        gram_b = (
            gram_pair + low + jnp.where(row_id < 2 * wanted, low.T, 0.0)
        )
        cross = (
            cross_pair
            + pad_rows(border[pair][wanted:], 2 * wanted)
            + pad_rows(border[third], 2 * wanted).T
        )
        gram_a = 0.5 * (cross + cross.T)
        shifted = cutoff[0] * eye - dot(gram_a, full_inv)
        square = dot(shifted, shifted)
        trace = jnp.sum(
            jnp.sum(jnp.where(row_id == col_id, square, 0.0), axis=1, keepdims=True),
            axis=0,
            keepdims=True,
        )
        norm = 1.0 / jnp.sqrt(trace + 1e-06)
        sign = (1.5 * norm) * shifted - (0.5 * norm) * dot(
            shifted * norm, square * norm
        )

        def newton(_, now):
            full = pad_rows(now)
            return 1.5 * now - 0.5 * dot(now, pad_rows(dot(now, full)))

        sign = lax.fori_loop(0, NS_STEPS - 1, newton, sign[0 : 3 * wanted])
        coeffs = 0.5 * (eye[0:wanted] + sign[0:wanted])
        mixed = jnp.concatenate([coeffs, jnp.where(narrow, 0.0, coeffs)], 0)
        basis[pair] = dot(mixed, basis[...])
        image[pair] = dot(mixed, image[...])

        @pl.when(turn + 1 < ITERS)
        def _():
            moved[0:wanted] = basis[0:wanted] - image[0:wanted]
            start_gather(turn + 3, moved, 0)

        square_mix = pad_rows(mixed)
        gram_ref[...] = dot_nt(dot(square_mix, gram_b), square_mix)
        cross_ref[...] = dot_nt(dot(square_mix, cross), square_mix)
        return carry

    lax.fori_loop(0, ITERS, iteration, 0)
    find_residual()
    out_x[...] = basis[0:wanted]
    out_p[...] = basis[wanted : 2 * wanted]
    out_r[...] = basis[third]
    out_ip[...] = image[wanted : 2 * wanted]


def hand_on(*refs):
    for source, target in zip(refs[:4], refs[4:]):
        target[...] = source[...]


def local(
    n_row, n_col,
    blocks, pattern_rows, pattern_cols, live_count, degree_scale, eigen_block, direction, cutoff,
):
    block_set = blocks[0, 0]
    slots, side, _ = block_set.shape
    wanted, docs = eigen_block.shape
    piece = docs // side
    out_rows = n_col * piece
    phases = ITERS + 2
    height = LANES // n_col
    bf16, f32 = jnp.bfloat16, jnp.float32
    sem = pltpu.SemaphoreType.DMA
    vmem = pl.BlockSpec(memory_space=pltpu.VMEM)
    smem = pl.BlockSpec(memory_space=pltpu.SMEM)
    out = jax.ShapeDtypeStruct((wanted, docs), f32)
    results = pl.pallas_call(
        functools.partial(body, n_row, n_col, piece, slots, wanted),
        out_shape=(out, out, out, out),
        in_specs=[smem, smem, smem, smem, pl.BlockSpec(memory_space=pl.ANY), vmem, vmem, vmem],
        out_specs=(vmem, vmem, vmem, vmem),
        scratch_shapes=[
            pltpu.SMEM((slots,), jnp.int32),
            pltpu.SMEM((out_rows,), jnp.int32),
            pltpu.VMEM((slots, side, side), bf16),
            pltpu.VMEM((LANES, docs), f32),
            pltpu.VMEM((LANES, docs), f32),
            pltpu.VMEM((wanted, docs), f32),
            pltpu.VMEM((n_row * piece, wanted, side), bf16),
            pltpu.VMEM((slots + 1, wanted, side), f32),
            pltpu.VMEM((phases, n_row * piece, wanted, side), bf16),
            pltpu.VMEM((phases, n_col - 1, piece, wanted, side), bf16),
            pltpu.VMEM((phases, n_col - 1, piece, wanted, side), bf16),
            pltpu.VMEM((phases, piece, wanted, side), f32),
            pltpu.VMEM((ITERS, n_col, height, LANES), f32),
            pltpu.VMEM((ITERS, n_col, height, LANES), f32),
            pltpu.VMEM((ITERS, n_row, height, LANES), f32),
            pltpu.VMEM((ITERS, n_col, height, LANES), f32),
            pltpu.VMEM((1, n_col, 2 * wanted, LANES), f32),
            pltpu.VMEM((1, n_row, 2 * wanted, LANES), f32),
            pltpu.VMEM((LANES, LANES), f32),
            pltpu.VMEM((LANES, LANES), f32),
            sem,
            sem((phases, n_row - 1)),
            sem((phases, n_row - 1)),
            sem((phases, n_col - 1)),
            sem((phases, n_col - 1)),
            sem((ITERS, n_col - 1)),
            sem((ITERS, n_col - 1)),
            sem((ITERS, n_row - 1)),
            sem((ITERS, n_row - 1)),
            sem((ITERS, n_col - 1)),
            sem((ITERS, n_col - 1)),
            sem((1, n_col - 1)),
            sem((1, n_col - 1)),
            sem((1, n_row - 1)),
            sem((1, n_row - 1)),
        ],
        compiler_params=pltpu.CompilerParams(
            collective_id=0, has_side_effects=True, vmem_limit_bytes=56 * 1024 * 1024
        ),
    )(pattern_rows[0, 0], pattern_cols[0, 0], live_count, cutoff, block_set, degree_scale, eigen_block, direction)
    return pl.pallas_call(
        hand_on,
        out_shape=(out, out, out, out),
        in_specs=[vmem] * 4,
        out_specs=(vmem, vmem, vmem, vmem),
    )(*results)


def solution(mesh):
    placed = (
        P("brow", "bcol", None, None, None),
        P("brow", "bcol", None),
        P("brow", "bcol", None),
        P("brow", "bcol"),
        P(("brow", "bcol")),
        P(None, ("brow", "bcol")),
        P(None, ("brow", "bcol")),
        P(),
    )
    return jax.shard_map(
        functools.partial(local, mesh.shape["brow"], mesh.shape["bcol"]),
        mesh=mesh,
        in_specs=placed,
        out_specs=(
            P(None, ("brow", "bcol")),
            P(None, ("brow", "bcol")),
            P(None, ("brow", "bcol")),
            P(None, ("brow", "bcol")),
        ),
        check_vma=False,
    )
```

```python
import functools

import jax
import jax.numpy as jnp
from jax import lax
from jax.experimental import pallas as pl
from jax.experimental.pallas import tpu as pltpu
from jax.sharding import PartitionSpec as P

ITERS = 2
NS_STEPS = 8
MESH = pl.DeviceIdType.MESH
LANES = 128


def halves(value):
    high = value.astype(jnp.bfloat16)
    return high, (value - high.astype(jnp.float32)).astype(jnp.bfloat16)


def split_dot(left, right, right_dim):
    rows = left.shape[0]
    left_high, left_low = halves(left)
    right_high, right_low = halves(right)

    def part(first, second):
        return lax.dot_general(
            first,
            second,
            (((1,), (right_dim,)), ((), ())),
            preferred_element_type=jnp.float32,
        )

    main = part(jnp.concatenate([left_high, left_low], 0), right_high)
    return main[:rows] + (main[rows:] + part(left_high, right_low))


def dot(left, right):
    return split_dot(left, right, 0)


def dot_nt(left, right):
    return split_dot(left, right, 1)


def grid_ids(rows):
    shape = (rows, LANES)
    return (
        lax.broadcasted_iota(jnp.int32, shape, 0),
        lax.broadcasted_iota(jnp.int32, shape, 1),
    )


def pad_rows(value, before=0):
    parts = [value, jnp.zeros((LANES - before - value.shape[0], LANES), jnp.float32)]
    if before:
        parts.insert(0, jnp.zeros((before, LANES), jnp.float32))
    return jnp.concatenate(parts, 0)


def inverse_pair(a, b, d):
    scale = 1.0 / (a * d - b * b)
    return d * scale, -(b * scale), a * scale


def inverse_four(m):
    p, q, r = inverse_pair(m[0][0], m[0][1], m[1][1])
    e = [[p * m[0][2 + c] + q * m[1][2 + c] for c in range(2)],
         [q * m[0][2 + c] + r * m[1][2 + c] for c in range(2)]]

    def schur(i, j):
        return m[2 + i][2 + j] - (m[0][2 + i] * e[0][j] + m[1][2 + i] * e[1][j])

    x, y, z = inverse_pair(schur(0, 0), schur(0, 1), schur(1, 1))
    f = [[e[i][0] * x + e[i][1] * y, e[i][0] * y + e[i][1] * z] for i in range(2)]

    def corner(i, j):
        return f[i][0] * e[j][0] + f[i][1] * e[j][1]

    off = q + corner(0, 1)
    return [
        [p + corner(0, 0), off, -f[0][0], -f[0][1]],
        [off, r + corner(1, 1), -f[1][0], -f[1][1]],
        [-f[0][0], -f[1][0], x, y],
        [-f[0][1], -f[1][1], y, z],
    ]


def inverse(matrix):
    side = matrix.shape[0]
    row_id, col_id = grid_ids(side)
    width = 4
    assert side % width == 0

    def sweep(step, now):
        first = step * width
        at_row = [row_id == first + k for k in range(width)]
        at_col = [col_id == first + k for k in range(width)]
        cols = [
            jnp.sum(jnp.where(at_col[k], now, 0.0), axis=1, keepdims=True)
            for k in range(width)
        ]
        rows = [
            jnp.sum(jnp.where(at_row[k], now, 0.0), axis=0, keepdims=True)
            for k in range(width)
        ]
        wide = [jnp.broadcast_to(col, now.shape) for col in cols]
        pivots = [
            [
                jnp.sum(jnp.where(at_row[i], wide[j], 0.0), axis=0, keepdims=True)
                for j in range(width)
            ]
            for i in range(width)
        ]
        inner = inverse_four(pivots)
        scaled_rows = [
            (inner[i][0] * rows[0] + inner[i][1] * rows[1])
            + (inner[i][2] * rows[2] + inner[i][3] * rows[3])
            for i in range(width)
        ]
        out = now - (
            (wide[0] * scaled_rows[0] + wide[1] * scaled_rows[1])
            + (wide[2] * scaled_rows[2] + wide[3] * scaled_rows[3])
        )
        for i in range(width):
            scaled_col = (wide[0] * inner[0][i] + wide[1] * inner[1][i]) + (
                wide[2] * inner[2][i] + wide[3] * inner[3][i]
            )
            out = jnp.where(at_col[i], scaled_col, out)
        for i in range(width):
            line = scaled_rows[i]
            for j in range(width):
                line = jnp.where(at_col[j][0:1], -inner[i][j], line)
            out = jnp.where(at_row[i], line, out)
        return out

    return -lax.fori_loop(0, side // width, sweep, matrix, unroll=2)


def extend_inverse(known, border, offset):
    side = border.shape[0]
    row_id, col_id = grid_ids(side)
    placed = (col_id == row_id + offset).astype(jnp.float32)
    edge = pad_rows(placed - dot(border, known))
    middle = inverse(dot_nt(border, edge))
    return known + dot(edge.T, pad_rows(dot(middle, edge)))


def body(
    n_row, n_col, piece, slots, wanted,
    row_table, col_table, live_ref, cutoff, blocks_hbm, scale_ref, eigen_ref, direction_ref,
    out_x, out_p, out_r, out_ip,
    prev_table, last_table, blocks, basis, image, moved, work, sums, gather, part, land, kept,
    own_x, cols_x, rows_x, all_x, pair_cols, pair_rows, gram_ref, cross_ref,
    block_sem, g_send, g_recv, p_send, p_recv,
    c_send, c_recv, r_send, r_recv, a_send, a_recv, d_send, d_recv, e_send, e_recv,
):
    me_row, me_col = lax.axis_index("brow"), lax.axis_index("bcol")
    side = blocks.shape[-1]
    block_copy = pltpu.make_async_copy(blocks_hbm, blocks, block_sem)
    block_copy.start()

    def row_peer(step):
        return lax.rem(me_row + step, n_row)

    def col_peer(step):
        return lax.rem(me_col + step, n_col)

    barrier = pltpu.get_barrier_semaphore()
    for step in range(1, n_row):
        pl.semaphore_signal(
            barrier, inc=1, device_id=(row_peer(step), me_col), device_id_type=MESH
        )
    for step in range(1, n_col):
        pl.semaphore_signal(
            barrier, inc=1, device_id=(me_row, col_peer(step)), device_id_type=MESH
        )

    scale = scale_ref[...].reshape(1, piece * side)
    basis[0:wanted] = eigen_ref[...]
    basis[wanted : 2 * wanted] = direction_ref[...]
    basis[2 * wanted :] = jnp.zeros((LANES - 2 * wanted, piece * side), jnp.float32)
    image[...] = jnp.zeros(image.shape, jnp.float32)
    sums[slots] = jnp.zeros(sums.shape[1:], jnp.float32)

    pl.semaphore_wait(barrier, n_row + n_col - 2)
    row_id, col_id = grid_ids(LANES)
    eye = jnp.where((row_id == col_id) & (row_id < 3 * wanted), 1.0, 0.0)

    def remote(src, dst, send, recv, device):
        return pltpu.make_async_remote_copy(
            src_ref=src, dst_ref=dst, send_sem=send, recv_sem=recv,
            device_id=device, device_id_type=MESH,
        )

    def spot(p):
        return slice(p * side, (p + 1) * side)

    def gather_copies(phase):
        mine = pl.ds(me_row * piece, piece)
        return [
            remote(
                gather.at[phase, mine], gather.at[phase, mine],
                g_send.at[phase, step - 1], g_recv.at[phase, step - 1],
                (row_peer(step), me_col),
            )
            for step in range(1, n_row)
        ]

    def start_gather(phase, panel, first):
        for p in range(piece):
            gather[phase, me_row * piece + p] = (
                scale[:, spot(p)] * panel[first : first + wanted, spot(p)]
            ).astype(jnp.bfloat16)
        for copy in gather_copies(phase):
            copy.start()

    def finish_gather(phase):
        for copy in gather_copies(phase):
            copy.wait()

        def move(k, carry):
            work[k] = gather[phase, k]
            return carry

        lax.fori_loop(0, n_row * piece, move, 0, unroll=4)

    def latest(row, bound):
        limit = jnp.minimum(bound, live_ref[0, 0])
        found = jnp.int32(slots)
        for k in range(slots):
            found = jnp.where((row_table[k] == row) & (k < limit), jnp.int32(k), found)
        return found

    def fill_previous(s, carry):
        prev_table[s] = latest(row_table[s], s)
        return carry

    def fill_last(row, carry):
        last_table[row] = latest(row, slots)
        return carry

    def turn_block(s, carry):
        blocks[s] = blocks[s].T
        return carry

    def multiply():
        group = 4
        assert slots % group == 0

        def some(step, carry):
            products = [
                lax.dot_general(
                    work[col_table[step * group + k]],
                    blocks[step * group + k],
                    (((1,), (0,)), ((), ())),
                    preferred_element_type=jnp.float32,
                )
                for k in range(group)
            ]
            for k in range(group):
                sums[step * group + k] = products[k] + sums[prev_table[step * group + k]]
            return carry

        lax.fori_loop(0, slots // group, some, 0, unroll=2)

    def scatter_copies(phase):
        return [
            remote(
                part.at[phase, step - 1], land.at[phase, step - 1],
                p_send.at[phase, step - 1], p_recv.at[phase, step - 1],
                (me_row, col_peer(step)),
            )
            for step in range(1, n_col)
        ]

    def fill_scatter(phase, start):
        copies = scatter_copies(phase) if start else []
        for step in range(1, n_col):
            owner = col_peer(step)
            for p in range(piece):
                part[phase, step - 1, p] = sums[last_table[owner * piece + p]].astype(
                    jnp.bfloat16
                )
            if start:
                copies[step - 1].start()
        for p in range(piece):
            kept[phase, p] = sums[last_table[me_col * piece + p]]

    def finish_scatter(phase, panel, first, target):
        for copy in scatter_copies(phase):
            copy.wait()
        for p in range(piece):
            total = kept[phase, p]
            for step in range(1, n_col):
                total = total + land[phase, step - 1, p].astype(jnp.float32)
            image[target : target + wanted, spot(p)] = (
                panel[first : first + wanted, spot(p)] - scale[:, spot(p)] * total
            )

    def swap_copies(turn, land, send, recv, along_col, source):
        me = me_col if along_col else me_row
        copies = []
        for step in range(1, n_col if along_col else n_row):
            peer = col_peer(step) if along_col else row_peer(step)
            device = (me_row, peer) if along_col else (peer, me_col)
            copies.append(
                remote(
                    source(peer), land.at[turn, me],
                    send.at[turn, step - 1], recv.at[turn, step - 1], device,
                )
            )
        return copies

    def swap(*args):
        copies = swap_copies(*args)
        for copy in copies:
            copy.start()
        for copy in copies:
            copy.wait()

    def total_of(land, turn, count):
        value = land[turn, 0]
        for k in range(1, count):
            value = value + land[turn, k]
        return value

    def add_up(turn, value):
        height = LANES // n_col
        for k in range(n_col):
            own_x[turn, k] = value[k * height : (k + 1) * height]
        cols_x[turn, me_col] = own_x[turn, me_col]
        swap(turn, cols_x, c_send, c_recv, True, lambda peer: own_x.at[turn, peer])
        rows_x[turn, me_row] = total_of(cols_x, turn, n_col)
        swap(turn, rows_x, r_send, r_recv, False, lambda peer: rows_x.at[turn, me_row])
        all_x[turn, me_col] = total_of(rows_x, turn, n_row)
        swap(turn, all_x, a_send, a_recv, True, lambda peer: all_x.at[turn, me_col])
        return jnp.concatenate([all_x[turn, k] for k in range(n_col)], 0)

    pair = slice(0, 2 * wanted)
    third = slice(2 * wanted, 3 * wanted)
    narrow = grid_ids(wanted)[1] < wanted
    half = grid_ids(wanted)[1] < 2 * wanted

    start_gather(0, basis, 0)
    lax.fori_loop(0, slots, fill_previous, 0)
    lax.fori_loop(0, n_col * piece, fill_last, 0)
    block_copy.wait()
    lax.fori_loop(0, slots, turn_block, 0, unroll=2)
    finish_gather(0)
    start_gather(1, basis, wanted)
    multiply()
    fill_scatter(0, True)
    finish_gather(1)
    multiply()
    fill_scatter(1, False)
    finish_scatter(0, basis, 0, 0)
    moved[0:wanted] = basis[0:wanted] - image[0:wanted]
    start_gather(2, moved, 0)
    for copy in scatter_copies(1):
        copy.start()
    finish_scatter(1, basis, wanted, wanted)

    def pair_swap():
        return swap_copies(
            0, pair_cols, d_send, d_recv, True, lambda peer: pair_cols.at[0, me_col]
        )

    both = jnp.concatenate([basis[pair], image[pair]], 0)
    pair_cols[0, me_col] = dot_nt(basis[pair], both)
    for copy in pair_swap():
        copy.start()

    def find_residual():
        gram_inv = pad_rows(inverse(jnp.where(narrow, gram_ref[0:wanted], 0.0)))
        rayleigh_t = jnp.where(narrow, cross_ref[...].T[0:wanted], 0.0)
        quotient_t = dot(rayleigh_t, gram_inv)
        quotient_t = quotient_t[:, :wanted]
        basis[third] = image[0:wanted] - dot(quotient_t, basis[0:wanted])
        return gram_inv, quotient_t

    def iteration(turn, carry):
        finish_gather(turn + 2)
        multiply()
        fill_scatter(turn + 2, True)

        @pl.when(turn == 0)
        def _():
            for copy in pair_swap():
                copy.wait()
            pair_rows[0, me_row] = total_of(pair_cols, 0, n_col)
            swap(0, pair_rows, e_send, e_recv, False, lambda peer: pair_rows.at[0, me_row])
            grams = pad_rows(total_of(pair_rows, 0, n_row))
            gram_ref[...] = jnp.where(col_id < 2 * wanted, grams, 0.0)
            cross_ref[...] = pad_rows(grams.T[2 * wanted :]).T

        gram_inv, quotient_t = find_residual()
        gram_pair = gram_ref[...]
        cross_pair = cross_ref[...]
        pair_inv = extend_inverse(
            gram_inv, jnp.where(half, gram_pair[wanted : 2 * wanted], 0.0), wanted
        )
        turned = basis[third] + dot(quotient_t, moved[...])
        by_residual = dot_nt(basis[third], jnp.concatenate([basis[...], image[...]], 0))
        finish_scatter(turn + 2, moved, 0, 2 * wanted)
        image[third] = turned - image[third]
        border = add_up(
            turn,
            pad_rows(
                jnp.concatenate(
                    [
                        by_residual[:, :LANES],
                        jnp.where(half, by_residual[:, LANES:], 0.0),
                        dot_nt(image[third], basis[...]),
                    ],
                    0,
                )
            ),
        )

        full_inv = extend_inverse(pair_inv, border[0:wanted], 2 * wanted)
        low = pad_rows(border[0:wanted], 2 * wanted)
        gram_b = (
            gram_pair + low + jnp.where(row_id < 2 * wanted, low.T, 0.0)
        )
        cross = (
            cross_pair
            + pad_rows(border[pair][wanted:], 2 * wanted)
            + pad_rows(border[third], 2 * wanted).T
        )
        gram_a = 0.5 * (cross + cross.T)
        shifted = cutoff[0] * eye - dot(gram_a, full_inv)
        square = dot(shifted, shifted)
        trace = jnp.sum(
            jnp.sum(jnp.where(row_id == col_id, square, 0.0), axis=1, keepdims=True),
            axis=0,
            keepdims=True,
        )
        norm = 1.0 / jnp.sqrt(trace + 1e-06)
        sign = (1.5 * norm) * shifted - (0.5 * norm) * dot(
            shifted * norm, square * norm
        )

        def newton(_, now):
            full = pad_rows(now)
            return 1.5 * now - 0.5 * dot(now, pad_rows(dot(now, full)))

        sign = lax.fori_loop(0, NS_STEPS - 1, newton, sign[0 : 3 * wanted], unroll=7)
        coeffs = 0.5 * (eye[0:wanted] + sign[0:wanted])
        mixed = jnp.concatenate([coeffs, jnp.where(narrow, 0.0, coeffs)], 0)
        basis[pair] = dot(mixed, basis[...])
        image[pair] = dot(mixed, image[...])

        @pl.when(turn + 1 < ITERS)
        def _():
            moved[0:wanted] = basis[0:wanted] - image[0:wanted]
            start_gather(turn + 3, moved, 0)

        square_mix = pad_rows(mixed)
        gram_ref[...] = dot_nt(dot(square_mix, gram_b), square_mix)
        cross_ref[...] = dot_nt(dot(square_mix, cross), square_mix)
        return carry

    lax.fori_loop(0, ITERS, iteration, 0)
    find_residual()
    out_x[...] = basis[0:wanted]
    out_p[...] = basis[wanted : 2 * wanted]
    out_r[...] = basis[third]
    out_ip[...] = image[wanted : 2 * wanted]


def hand_on(*refs):
    for source, target in zip(refs[:4], refs[4:]):
        target[...] = source[...]


def local(
    n_row, n_col,
    blocks, pattern_rows, pattern_cols, live_count, degree_scale, eigen_block, direction, cutoff,
):
    block_set = blocks[0, 0]
    slots, side, _ = block_set.shape
    wanted, docs = eigen_block.shape
    piece = docs // side
    out_rows = n_col * piece
    phases = ITERS + 2
    height = LANES // n_col
    bf16, f32 = jnp.bfloat16, jnp.float32
    sem = pltpu.SemaphoreType.DMA
    vmem = pl.BlockSpec(memory_space=pltpu.VMEM)
    smem = pl.BlockSpec(memory_space=pltpu.SMEM)
    out = jax.ShapeDtypeStruct((wanted, docs), f32)
    results = pl.pallas_call(
        functools.partial(body, n_row, n_col, piece, slots, wanted),
        out_shape=(out, out, out, out),
        in_specs=[smem, smem, smem, smem, pl.BlockSpec(memory_space=pl.ANY), vmem, vmem, vmem],
        out_specs=(vmem, vmem, vmem, vmem),
        scratch_shapes=[
            pltpu.SMEM((slots,), jnp.int32),
            pltpu.SMEM((out_rows,), jnp.int32),
            pltpu.VMEM((slots, side, side), bf16),
            pltpu.VMEM((LANES, docs), f32),
            pltpu.VMEM((LANES, docs), f32),
            pltpu.VMEM((wanted, docs), f32),
            pltpu.VMEM((n_row * piece, wanted, side), bf16),
            pltpu.VMEM((slots + 1, wanted, side), f32),
            pltpu.VMEM((phases, n_row * piece, wanted, side), bf16),
            pltpu.VMEM((phases, n_col - 1, piece, wanted, side), bf16),
            pltpu.VMEM((phases, n_col - 1, piece, wanted, side), bf16),
            pltpu.VMEM((phases, piece, wanted, side), f32),
            pltpu.VMEM((ITERS, n_col, height, LANES), f32),
            pltpu.VMEM((ITERS, n_col, height, LANES), f32),
            pltpu.VMEM((ITERS, n_row, height, LANES), f32),
            pltpu.VMEM((ITERS, n_col, height, LANES), f32),
            pltpu.VMEM((1, n_col, 2 * wanted, LANES), f32),
            pltpu.VMEM((1, n_row, 2 * wanted, LANES), f32),
            pltpu.VMEM((LANES, LANES), f32),
            pltpu.VMEM((LANES, LANES), f32),
            sem,
            sem((phases, n_row - 1)),
            sem((phases, n_row - 1)),
            sem((phases, n_col - 1)),
            sem((phases, n_col - 1)),
            sem((ITERS, n_col - 1)),
            sem((ITERS, n_col - 1)),
            sem((ITERS, n_row - 1)),
            sem((ITERS, n_row - 1)),
            sem((ITERS, n_col - 1)),
            sem((ITERS, n_col - 1)),
            sem((1, n_col - 1)),
            sem((1, n_col - 1)),
            sem((1, n_row - 1)),
            sem((1, n_row - 1)),
        ],
        compiler_params=pltpu.CompilerParams(
            collective_id=0, has_side_effects=True, vmem_limit_bytes=56 * 1024 * 1024
        ),
    )(pattern_rows[0, 0], pattern_cols[0, 0], live_count, cutoff, block_set, degree_scale, eigen_block, direction)
    return pl.pallas_call(
        hand_on,
        out_shape=(out, out, out, out),
        in_specs=[vmem] * 4,
        out_specs=(vmem, vmem, vmem, vmem),
    )(*results)


def solution(mesh):
    placed = (
        P("brow", "bcol", None, None, None),
        P("brow", "bcol", None),
        P("brow", "bcol", None),
        P("brow", "bcol"),
        P(("brow", "bcol")),
        P(None, ("brow", "bcol")),
        P(None, ("brow", "bcol")),
        P(),
    )
    return jax.shard_map(
        functools.partial(local, mesh.shape["brow"], mesh.shape["bcol"]),
        mesh=mesh,
        in_specs=placed,
        out_specs=(
            P(None, ("brow", "bcol")),
            P(None, ("brow", "bcol")),
            P(None, ("brow", "bcol")),
            P(None, ("brow", "bcol")),
        ),
        check_vma=False,
    )
```
